32 devices in a mesh: groups: 2 (over y), sub: 4 (over z), blk: 4 (over x, core).
Axes of the slice: x: 2, y: 2, z: 4, core: 2. Of those that a mesh axis runs over, the one named last changes fastest.
Arguments:
- conductance: float32 [128, 8192], P(('groups', 'sub'), 'blk'), parts along dimension 0, may hold values from 0.1 to 10
- source_mask: int32 [128, 8192], P(('groups', 'sub'), 'blk'), parts along dimension 0, may hold values 0 or 1
- ground_mask: int32 [128, 8192], P(('groups', 'sub'), 'blk'), parts along dimension 0, may hold values 0 or 1
- nodata_mask: int32 [128, 8192], P(('groups', 'sub'), 'blk'), parts along dimension 0, may hold values 0 or 1
Outputs:
- potential: float32 [128, 8192], P(('groups', 'sub'), 'blk'), parts along dimension 0
The draws below stay inside these ranges and needn't reach their ends.
There are 2 independent parts, one for each index of `groups`. The reference program is written for one: setup_inputs(seed, part) draws one part's arguments, and reference() takes and returns one part's arrays. A program takes and returns all parts, laid end to end along the dimension named above; each array names one. Nothing has to cross between parts.
All inputs are finite; a program needn't handle non-finite values. No bound on the sum of `source_mask` or of `ground_mask` or of `nodata_mask` on one device may be relied on, other than what follows from the above.
Results may differ from the reference program's by a relative error of at most 0.0003.
Values sent between devices are 32-bit elements; how exact they have to be, the bound alone decides.
A program may use at most 64 MiB of HBM per device.

```python
import math
import jax
import jax.numpy as jnp

LEVELS = 5
PRE_SWEEPS = 2
POST_SWEEPS = 2
COARSE_SWEEPS = 10
GRID_ROWS = 64
GRID_COLS = 8192


def set_ends(drawn, key, smallest, largest):
    longest = drawn.shape.index(max(drawn.shape))
    spots = []
    for shift in (0, 1):
        where = [jax.random.randint(jax.random.fold_in(key, axis), (), 0, length) for axis, length in enumerate(drawn.shape)]
        where[longest] = (where[longest] + shift) % drawn.shape[longest]
        spots.append(tuple(where))
    return drawn.at[spots[0]].set(smallest).at[spots[1]].set(largest)


def steps_of(own_key, shape, cuts, low, largest):
    gain, own = 1.0, jax.random.fold_in(own_key, 6)
    for dim, parts in cuts:
        steps = jnp.exp(jax.random.uniform(jax.random.fold_in(own, dim), (parts,), jnp.float32, low / len(cuts), largest / len(cuts)))
        gain = gain * jnp.repeat(steps, shape[dim] // parts).reshape([-1 if axis == dim else 1 for axis in range(len(shape))])
    return gain


def setup_inputs(seed: int = 0, part: int = 0) -> dict:
    streams_of = jax.random.split(jax.random.key(seed), 5)
    part_splits = jax.random.split(jax.random.fold_in(streams_of[4], part), 5)
    return {
        "conductance": jnp.clip(jnp.exp(math.log(10.0) - 4.6051702 * jax.random.uniform(part_splits[0], (GRID_ROWS, GRID_COLS), jnp.float32) ** steps_of(part_splits[0], (GRID_ROWS, GRID_COLS), ((0, 4), (1, 4)), -0.2, 0.2)), 0.1, 10.0),
        "source_mask": set_ends((jax.random.randint(part_splits[1], (GRID_ROWS, GRID_COLS), 0, 8) < 1).astype(jnp.int32), jax.random.fold_in(part_splits[1], 1), 0, 1),
        "ground_mask": set_ends((jax.random.randint(part_splits[2], (GRID_ROWS, GRID_COLS), 0, 1024) < 1).astype(jnp.int32), jax.random.fold_in(part_splits[2], 1), 0, 1),
        "nodata_mask": set_ends((jax.random.randint(part_splits[3], (GRID_ROWS, GRID_COLS), 0, 16) < 1).astype(jnp.int32), jax.random.fold_in(part_splits[3], 1), 0, 1),
    }


smooth_low = 0.5
smooth_high = 2.0
coarse_low = 0.02
coarse_high = 2.0


def chebyshev_terms(sweep_count, low_end, high_end):
    mid_point = 0.5 * (high_end + low_end)
    half_width = 0.5 * (high_end - low_end)
    sigma_value = mid_point / half_width
    rho_value = 1.0 / sigma_value
    coefficients = [(0.0, 1.0 / mid_point)]
    for step_index in range(1, sweep_count):
        rho_next = 1.0 / (2.0 * sigma_value - rho_value)
        coefficients.append((rho_next * rho_value, 2.0 * rho_next / half_width))
        rho_value = rho_next
    return coefficients


def pad_zero(field):
    return jnp.pad(field, 1)


def neighbor_of(padded, row_shift, col_shift):
    row_total = padded.shape[0]
    col_total = padded.shape[1]
    return padded[1 + row_shift:row_total - 1 + row_shift, 1 + col_shift:col_total - 1 + col_shift]


shifts_list = ((1, 0), (-1, 0), (0, 1), (0, -1))


def level_operator(cond_level, ground_admit, padded_cond):
    validity = jnp.where(cond_level > 0.0, 1.0, 0.0).astype(jnp.float32)
    padded_valid = jnp.where(padded_cond > 0.0, 1.0, 0.0).astype(jnp.float32)
    edges = []
    for row_shift, col_shift in shifts_list:
        other_cond = neighbor_of(padded_cond, row_shift, col_shift)
        other_valid = neighbor_of(padded_valid, row_shift, col_shift)
        edges.append(validity * other_valid * 0.5 * (cond_level + other_cond))
    diagonal = edges[0] + edges[1] + edges[2] + edges[3] + ground_admit + (1.0 - validity)
    precond = jnp.maximum(diagonal, 0.25 * cond_level)
    return (tuple(edges), diagonal, precond, validity)


def apply_operator(operator, padded_field, field):
    result = operator[1] * field
    for edge_index in range(4):
        row_shift, col_shift = shifts_list[edge_index]
        result = result - operator[0][edge_index] * neighbor_of(padded_field, row_shift, col_shift)
    return result


def smooth(operator, padder, source_term, iterate, coefficients):
    update = None
    for keep_part, fresh_part in coefficients:
        if iterate is None:
            residual = source_term
            iterate = jnp.zeros_like(source_term)
        else:
            residual = source_term - apply_operator(operator, padder(iterate), iterate)
        scaled = residual / operator[2]
        if update is None:
            update = fresh_part * scaled
        else:
            update = keep_part * update + fresh_part * scaled
        iterate = iterate + update
    return iterate


def coarsen_sum(field):
    return field.reshape(field.shape[0] // 2, 2, field.shape[1] // 2, 2).sum(axis=(1, 3))


def prolong(field):
    return jnp.repeat(jnp.repeat(field, 2, axis=0), 2, axis=1)


def reference(conductance, source_mask, ground_mask, nodata_mask):
    validity = 1.0 - nodata_mask.astype(jnp.float32)
    cond_level = conductance * validity
    ground_admit = ground_mask.astype(jnp.float32) * cond_level
    right_side = validity * (source_mask.astype(jnp.float32) - 0.125)
    pre_terms = chebyshev_terms(PRE_SWEEPS, smooth_low, smooth_high)
    post_terms = chebyshev_terms(POST_SWEEPS, smooth_low, smooth_high)
    stored = []
    for level_index in range(LEVELS - 1):
        operator = level_operator(cond_level, ground_admit, pad_zero(cond_level))
        iterate = smooth(operator, pad_zero, right_side, None, pre_terms)
        residual = right_side - apply_operator(operator, pad_zero(iterate), iterate)
        stored.append((operator, right_side, iterate))
        right_side = coarsen_sum(residual)
        cond_level = 0.25 * coarsen_sum(cond_level)
        ground_admit = coarsen_sum(ground_admit)
    operator = level_operator(cond_level, ground_admit, pad_zero(cond_level))
    iterate = smooth(operator, pad_zero, right_side, None, chebyshev_terms(COARSE_SWEEPS, coarse_low, coarse_high))
    for level_index in reversed(range(LEVELS - 1)):
        operator, right_side, previous = stored[level_index]
        iterate = previous + operator[3] * prolong(iterate)
        iterate = smooth(operator, pad_zero, right_side, iterate, post_terms)
    return iterate
```

```python
import functools
import jax
import jax.numpy as jnp
from jax import lax
from jax.experimental import pallas as pl
from jax.experimental.pallas import tpu as pltpu
from jax.sharding import PartitionSpec as P

LEVELS = 5
SMOOTH = (2, 0.5, 2.0)
COARSE_LOW, COARSE_HIGH = 0.02, 2.0
DIRS = ((-1, 0), (1, 0), (0, -1), (0, 1), (-1, -1), (-1, 1), (1, -1), (1, 1))
MESH = pl.DeviceIdType.MESH


def round_up(n, k):
    return -(-n // k) * k


def chebyshev_terms(sweep_count, low_end, high_end):
    mid = 0.5 * (high_end + low_end)
    half = 0.5 * (high_end - low_end)
    sigma = mid / half
    rho = 1.0 / sigma
    terms = [(0.0, 1.0 / mid)]
    for _ in range(1, sweep_count):
        rho_next = 1.0 / (2.0 * sigma - rho)
        terms.append((rho_next * rho, 2.0 * rho_next / half))
        rho = rho_next
    return terms


def rolled(x, shift, axis):
    return pltpu.roll(x, shift % x.shape[axis], axis)


def level_operator(c, g, whole_rows):
    rows, cols = c.shape
    h = 0.5 * c
    valid = c > 0.0
    c_r = rolled(c, -1, 1)
    c_d = rolled(c, -1, 0)
    e_r = jnp.where(valid & (c_r > 0.0), h + 0.5 * c_r, 0.0)
    ok_d = valid & (c_d > 0.0)
    if whole_rows:
        ok_d = ok_d & (lax.broadcasted_iota(jnp.int32, c.shape, 0) < rows - 1)
    e_d = jnp.where(ok_d, h + 0.5 * c_d, 0.0)
    e_l = rolled(e_r, 1, 1)
    e_u = rolled(e_d, 1, 0)
    m = jnp.where(valid, 1.0, 0.0)
    diag = e_d + e_u + e_r + e_l + g + (1.0 - m)
    inv = 1.0 / jnp.maximum(diag, 0.25 * c)
    return e_r, e_l, e_d, e_u, diag, inv, m


def residual(op, f, x):
    e_r, e_l, e_d, e_u, diag, inv, m = op
    out = f - diag * x
    out = out + e_r * rolled(x, -1, 1) + e_l * rolled(x, 1, 1)
    return out + e_d * rolled(x, -1, 0) + e_u * rolled(x, 1, 0)


def smooth(op, f, x, terms):
    d = None
    for keep, fresh in terms:
        r = f if x is None else residual(op, f, x)
        step = fresh * (r * op[5])
        d = step if d is None else keep * d + step
        x = d if x is None else x + d
    return x


def split_dot(x, w):
    hi = x.astype(jnp.bfloat16)
    lo = (x - hi.astype(jnp.float32)).astype(jnp.bfloat16)
    return jnp.dot(hi, w, preferred_element_type=jnp.float32) + jnp.dot(
        lo, w, preferred_element_type=jnp.float32
    )


def coarsen(x, tmp, pair):
    rows, cols = x.shape
    if cols % 256:
        x = jnp.concatenate([x, jnp.zeros((rows, 128), jnp.float32)], axis=1)
        cols += 128
    k = cols // 256
    stack = jnp.concatenate([x[:, 256 * j : 256 * j + 256] for j in range(k)], axis=0)
    tmp[: rows * k, :] = split_dot(stack, pair)
    n = rows * k // 2
    s = tmp[pl.ds(0, n, stride=2), :] + tmp[pl.ds(1, n, stride=2), :]
    half = rows // 2
    return [s[half * j : half * (j + 1)] for j in range(k)]


def prolong(x, tmp, pair_t, cols):
    rows = x.shape[0]
    k = x.shape[1] // 128
    for j in range(k):
        tile = x[:, 128 * j : 128 * j + 128]
        tmp[pl.ds(2 * rows * j, rows, stride=2), :] = tile
        tmp[pl.ds(2 * rows * j + 1, rows, stride=2), :] = tile
    out = split_dot(tmp[: 2 * rows * k, :], pair_t)
    out = [out[2 * rows * j : 2 * rows * (j + 1)] for j in range(k)]
    return jnp.concatenate(out, axis=1)[:, :cols]


def kernel(
    plan,
    cond, src, gnd, nod, out,
    c0, g0, f0, x0, c1, g1, f1, x1, c2, g2, f2, y2, f3, f4, tmp, tmp_up,
    a_row_s, a_row_r, a_col_s, a_col_r, a_cor_s, a_cor_r, a_sem,
    x0_s, x0_r, cg1_s, cg1_r, f1_s, f1_r, x1_s, x1_r, row_sem,
    cg2_g, f2_g, gather_sem,
):
    n_sub, n_blk, halo, widths, coarse_count = plan
    s, b = lax.axis_index("sub"), lax.axis_index("blk")
    w0, w1, w2, w3, w4 = widths
    own = out.shape[1]

    def exists(dr, dc):
        ok = None
        for need, cond_ in (
            (dr < 0, s > 0), (dr > 0, s < n_sub - 1), (dc < 0, b > 0), (dc > 0, b < n_blk - 1),
        ):
            if need:
                ok = cond_ if ok is None else ok & cond_
        return ok

    for ref in (c0, g0, f0, c1, g1, f1, y2, f3, f4):
        ref[...] = jnp.zeros_like(ref)

    barrier = pltpu.get_barrier_semaphore()
    for dr in range(n_sub):
        @pl.when(s != dr)
        def _():
            pl.semaphore_signal(barrier, 1, device_id={"sub": dr}, device_id_type=MESH)
    for dr, dc in DIRS[2:]:
        @pl.when(exists(dr, dc))
        def _():
            pl.semaphore_signal(
                barrier, 1, device_id={"sub": s + dr, "blk": b + dc}, device_id_type=MESH
            )

    valid = 1.0 - nod[...].astype(jnp.float32)
    c = cond[...] * valid
    g = gnd[...].astype(jnp.float32) * c
    f = valid * (src[...].astype(jnp.float32) - 0.125)
    c0[4:20, halo : halo + own] = c
    g0[4:20, halo : halo + own] = g
    f0[4:20, halo : halo + own] = f
    for i, (rc, rg) in enumerate(((slice(0, 3), slice(0, 2)), (slice(13, 16), slice(14, 16)))):
        a_row_s[i, 0:3] = c[rc]
        a_row_s[i, 3:5] = g[rg]
        a_row_s[i, 5:7] = f[rg]
        a_row_s[i, 7:8] = jnp.zeros((1, own), jnp.float32)
        for j, lanes in enumerate((slice(0, halo), slice(own - halo, own))):
            a_cor_s[2 * i + j, 0:3] = c[rc, lanes]
            a_cor_s[2 * i + j, 3:5] = g[rg, lanes]
            a_cor_s[2 * i + j, 5:7] = f[rg, lanes]
            a_cor_s[2 * i + j, 7:8] = jnp.zeros((1, halo), jnp.float32)
    for j, lanes in enumerate((slice(0, halo), slice(own - halo, own))):
        a_col_s[j, 0:16] = c[:, lanes]
        a_col_s[j, 16:32] = g[:, lanes]
        a_col_s[j, 32:48] = f[:, lanes]

    has = lambda flag: jnp.where(flag, 1, 0)
    partners = n_sub - 1
    for dr, dc in DIRS[2:]:
        partners = partners + has(exists(dr, dc))
    pl.semaphore_wait(barrier, partners)

    def remote(src_ref, dst_ref, send, recv, dr, dc=0):
        return pltpu.make_async_remote_copy(
            src_ref=src_ref, dst_ref=dst_ref, send_sem=send, recv_sem=recv,
            device_id={"sub": s + dr, "blk": b + dc}, device_id_type=MESH,
        )

    def a_copy(d):
        dr, dc = DIRS[d]
        if d < 2:
            pair_ = a_row_s.at[d], a_row_r.at[d]
        elif d < 4:
            pair_ = a_col_s.at[d - 2], a_col_r.at[d - 2]
        else:
            pair_ = a_cor_s.at[d - 4], a_cor_r.at[d - 4]
        return remote(*pair_, a_sem.at[0, d], a_sem.at[1, d], dr, dc)

    row_bufs = ((x0_s, x0_r), (cg1_s, cg1_r), (f1_s, f1_r), (x1_s, x1_r))

    def row_copy(e, d):
        send, recv = row_bufs[e]
        return remote(send.at[d], recv.at[d], row_sem.at[0, e, d], row_sem.at[1, e, d], DIRS[d][0])

    def row_start(e):
        for d in range(2):
            @pl.when(exists(*DIRS[d]))
            def _():
                row_copy(e, d).start()

    def row_wait(e, put):
        for d in range(2):
            @pl.when(exists(-DIRS[d][0], 0))
            def _():
                row_copy(e, d).wait_recv()
                put(d)

    def gather_copy(e, other, sender):
        buf = (cg2_g, f2_g)[e]
        return pltpu.make_async_remote_copy(
            src_ref=buf.at[sender], dst_ref=buf.at[sender],
            send_sem=gather_sem.at[0, e, other], recv_sem=gather_sem.at[1, e, sender],
            device_id={"sub": other}, device_id_type=MESH,
        )

    def gather_start(e):
        for other in range(n_sub):
            @pl.when(s != other)
            def _():
                gather_copy(e, other, s).start()

    def gather_wait(e):
        for other in range(n_sub):
            @pl.when(s != other)
            def _():
                gather_copy(e, other, other).wait_recv()

    for d in range(8):
        @pl.when(exists(*DIRS[d]))
        def _():
            a_copy(d).start()

    iota = lambda shape, dim: lax.broadcasted_iota(jnp.int32, shape, dim)
    pair = jnp.where(
        jnp.right_shift(iota((256, 128), 0), 1) == iota((256, 128), 1), 1.0, 0.0
    ).astype(jnp.bfloat16)
    pair_t = jnp.where(
        jnp.right_shift(iota((128, 256), 1), 1) == iota((128, 256), 0), 1.0, 0.0
    ).astype(jnp.bfloat16)

    for d, (dr, dc) in enumerate(DIRS):
        @pl.when(exists(-dr, -dc))
        def _():
            a_copy(d).wait_recv()
            lanes = {0: slice(halo, halo + own), 1: slice(0, halo), -1: slice(halo + own, w0)}[dc]
            if dr == 0:
                for k, ref in enumerate((c0, g0, f0)):
                    ref[4:20, lanes] = a_col_r[d - 2, 16 * k : 16 * k + 16]
            else:
                got = (a_row_r, d) if d < 2 else (a_cor_r, d - 4)
                got = got[0].at[got[1]]
                c0[slice(1, 4) if dr > 0 else slice(20, 23), lanes] = got[0:3]
                near = slice(2, 4) if dr > 0 else slice(20, 22)
                g0[near, lanes] = got[3:5]
                f0[near, lanes] = got[5:7]

    both = jnp.concatenate([0.25 * c0[4:20, :], g0[4:20, :]], axis=0)
    both = jnp.concatenate(coarsen(both, tmp, pair), axis=1)
    c1[4:12, :] = both[0:8]
    g1[4:12, :] = both[8:16]
    for i, (rc, rg) in enumerate(((slice(0, 3), slice(8, 10)), (slice(5, 8), slice(14, 16)))):
        cg1_s[i, 0:3] = both[rc]
        cg1_s[i, 3:5] = both[rg]
        cg1_s[i, 5:8] = jnp.zeros((3, w1), jnp.float32)
    row_start(1)
    both = jnp.concatenate([0.25 * both[0:8], both[8:16]], axis=0)
    both = jnp.concatenate(coarsen(both, tmp, pair), axis=1)
    cg2_g[s] = both
    gather_start(0)

    terms = chebyshev_terms(*SMOOTH)
    op0 = level_operator(c0[...], g0[...], False)
    f = f0[...]
    x = smooth(op0, f, None, terms)
    r = residual(op0, f, x)
    rhs = jnp.concatenate(coarsen(r[4:20], tmp, pair), axis=1)
    f1[4:12, :] = rhs
    f1_s[0] = rhs[0:2]
    f1_s[1] = rhs[6:8]
    row_start(2)
    x0[...] = x
    x0_s[0] = x[4:6]
    x0_s[1] = x[18:20]
    row_start(0)

    def put_cg1(d):
        c1[slice(12, 15) if d == 0 else slice(1, 4), :] = cg1_r[d, 0:3]
        g1[slice(12, 14) if d == 0 else slice(2, 4), :] = cg1_r[d, 3:5]

    row_wait(1, put_cg1)
    op1 = level_operator(c1[...], g1[...], False)

    def put_f1(d):
        f1[slice(12, 14) if d == 0 else slice(2, 4), :] = f1_r[d]

    row_wait(2, put_f1)
    fl1 = f1[...]
    x = smooth(op1, fl1, None, terms)
    r = residual(op1, fl1, x)
    f2_g[s] = jnp.concatenate(coarsen(r[4:12], tmp, pair), axis=1)
    gather_start(1)
    x1[...] = x
    x1_s[0] = x[4:7]
    x1_s[1] = x[9:12]
    row_start(3)

    gather_wait(0)
    for k in range(n_sub):
        c2[4 * k : 4 * k + 4, :] = cg2_g[k, 0:4]
        g2[4 * k : 4 * k + 4, :] = cg2_g[k, 4:8]

    cg = (c2[...], g2[...])
    ops = [level_operator(*cg, True)]
    rows = 4 * n_sub
    for level, width in ((3, w3), (4, w4)):
        rows //= 2
        full = max(rows, 8)
        parts = []
        for k, v in enumerate(cg):
            tiles = coarsen(0.25 * v if k == 0 else v, tmp, pair)
            v = jnp.concatenate(tiles, axis=1)[:rows]
            if full > rows:
                v = jnp.concatenate([v, jnp.zeros((full - rows, width), jnp.float32)], axis=0)
            parts.append(v)
        cg = tuple(parts)
        ops.append(level_operator(*cg, True))

    gather_wait(1)
    for k in range(n_sub):
        f2[4 * k : 4 * k + 4, :] = f2_g[k]
    rhs = f2[...]
    kept = []
    rows = 4 * n_sub
    for level in (2, 3):
        op = ops[level - 2]
        x = smooth(op, rhs, None, terms)
        r = residual(op, rhs, x)
        kept.append((rhs, x))
        rows //= 2
        ref = (f3, f4)[level - 2]
        for j, tile in enumerate(coarsen(r, tmp, pair)):
            ref[:rows, 128 * j : 128 * j + 128] = tile
        rhs = ref[...]
    y = smooth(ops[2], rhs, None, chebyshev_terms(coarse_count, COARSE_LOW, COARSE_HIGH))
    for level, width in ((3, w3), (2, w2)):
        op = ops[level - 2]
        rhs, x = kept[level - 2]
        rows = n_sub if level == 3 else 2 * n_sub
        y = x + op[6] * prolong(y[:rows], tmp_up, pair_t, width)
        y = smooth(op, rhs, y, terms)

    for k in range(n_sub):
        y2[k + 1] = y[4 * k : 4 * k + 4]
    y = jnp.concatenate([y2[s][2:4], y2[s + 1], y2[s + 2][0:2]], axis=0)

    def put_x1(d):
        x1[slice(12, 15) if d == 0 else slice(1, 4), :] = x1_r[d]

    row_wait(3, put_x1)
    y = x1[...] + op1[6] * prolong(y, tmp_up, pair_t, w1)
    y = smooth(op1, fl1, y, terms)

    def put_x0(d):
        x0[slice(20, 22) if d == 0 else slice(2, 4), :] = x0_r[d]

    row_wait(0, put_x0)
    y = x0[...] + op0[6] * prolong(y[2:14], tmp_up, pair_t, w0)
    y = smooth(op0, f0[...], y, terms)
    out[...] = y[4:20, halo : halo + own]

    for d in range(8):
        @pl.when(exists(*DIRS[d]))
        def _():
            a_copy(d).wait_send()
    for e in range(4):
        for d in range(2):
            @pl.when(exists(*DIRS[d]))
            def _():
                row_copy(e, d).wait_send()
    for e in range(2):
        for other in range(n_sub):
            @pl.when(s != other)
            def _():
                gather_copy(e, other, s).wait_send()


def body(conductance, source_mask, ground_mask, nodata_mask):
    n_sub, n_blk = lax.axis_size("sub"), lax.axis_size("blk")
    rows, own = conductance.shape
    assert rows == 16 and own % 256 == 0
    coarse_count = 8 + n_sub // 2
    need = coarse_count + 2
    for _ in range(LEVELS - 1):
        need = 2 * need + 2
    halo = round_up(need, 256)
    assert halo <= own
    w0 = own + 2 * halo
    widths = (w0,) + tuple(round_up(w0 >> l, 128) for l in range(1, 5))
    w1, w2, w3, w4 = widths[1:]
    f32 = lambda *shape: pltpu.VMEM(shape, jnp.float32)
    sem = lambda *shape: pltpu.SemaphoreType.DMA(shape)
    r2, r3, r4 = 4 * n_sub, max(2 * n_sub, 8), max(n_sub, 8)
    tmp_rows = max(32 * round_up(w0, 256) // 256, 4 * n_sub * round_up(w2, 256) // 256)
    up_rows = max(24 * w1 // 128, 4 * n_sub * w3 // 128)
    vmem = pl.BlockSpec(memory_space=pltpu.VMEM)
    return pl.pallas_call(
        functools.partial(kernel, (n_sub, n_blk, halo, widths, coarse_count)),
        out_shape=jax.ShapeDtypeStruct((rows, own), jnp.float32),
        in_specs=[vmem] * 4,
        out_specs=vmem,
        scratch_shapes=[
            f32(24, w0), f32(24, w0), f32(24, w0), f32(24, w0),
            f32(16, w1), f32(16, w1), f32(16, w1), f32(16, w1),
            f32(r2, w2), f32(r2, w2), f32(r2, w2), f32(n_sub + 2, 4, w2),
            f32(r3, w3), f32(r4, w4), f32(tmp_rows, 128), f32(up_rows, 128),
            f32(2, 8, own), f32(2, 8, own), f32(2, 48, halo), f32(2, 48, halo),
            f32(4, 8, halo), f32(4, 8, halo), sem(2, 8),
            f32(2, 2, w0), f32(2, 2, w0), f32(2, 8, w1), f32(2, 8, w1),
            f32(2, 2, w1), f32(2, 2, w1), f32(2, 3, w1), f32(2, 3, w1), sem(2, 4, 2),
            f32(n_sub, 8, w2), f32(n_sub, 4, w2), sem(2, 2, n_sub),
        ],
        compiler_params=pltpu.CompilerParams(
            collective_id=0, has_side_effects=True, vmem_limit_bytes=40 * 1024 * 1024
        ),
    )(conductance, source_mask, ground_mask, nodata_mask)


def solution(mesh):
    spec = P(("groups", "sub"), "blk")
    return jax.shard_map(
        body, mesh=mesh, in_specs=(spec,) * 4, out_specs=spec, check_vma=False
    )
```

```python
import functools
import jax
import jax.numpy as jnp
from jax import lax
from jax.experimental import pallas as pl
from jax.experimental.pallas import tpu as pltpu
from jax.sharding import PartitionSpec as P

LEVELS = 5
SMOOTH = (2, 0.5, 2.0)
COARSE_LOW, COARSE_HIGH = 0.02, 2.0
DIRS = ((-1, 0), (1, 0), (0, -1), (0, 1), (-1, -1), (-1, 1), (1, -1), (1, 1))
MESH = pl.DeviceIdType.MESH


def round_up(n, k):
    return -(-n // k) * k


def chebyshev_terms(sweep_count, low_end, high_end):
    mid = 0.5 * (high_end + low_end)
    half = 0.5 * (high_end - low_end)
    sigma = mid / half
    rho = 1.0 / sigma
    terms = [(0.0, 1.0 / mid)]
    for _ in range(1, sweep_count):
        rho_next = 1.0 / (2.0 * sigma - rho)
        terms.append((rho_next * rho, 2.0 * rho_next / half))
        rho = rho_next
    return terms


def rolled(x, shift, axis):
    return pltpu.roll(x, shift % x.shape[axis], axis)


def level_operator(c, g, whole_rows):
    rows, cols = c.shape
    h = 0.5 * c
    valid = c > 0.0
    c_r = rolled(c, -1, 1)
    c_d = rolled(c, -1, 0)
    e_r = jnp.where(valid & (c_r > 0.0), h + 0.5 * c_r, 0.0)
    ok_d = valid & (c_d > 0.0)
    if whole_rows:
        ok_d = ok_d & (lax.broadcasted_iota(jnp.int32, c.shape, 0) < rows - 1)
    e_d = jnp.where(ok_d, h + 0.5 * c_d, 0.0)
    e_l = rolled(e_r, 1, 1)
    e_u = rolled(e_d, 1, 0)
    m = jnp.where(valid, 1.0, 0.0)
    diag = e_d + e_u + e_r + e_l + g + (1.0 - m)
    inv = 1.0 / jnp.maximum(diag, 0.25 * c)
    return e_r, e_l, e_d, e_u, diag, inv, m


def residual(op, f, x):
    e_r, e_l, e_d, e_u, diag, inv, m = op
    out = f - diag * x
    out = out + e_r * rolled(x, -1, 1) + e_l * rolled(x, 1, 1)
    return out + e_d * rolled(x, -1, 0) + e_u * rolled(x, 1, 0)


def smooth(op, f, x, terms):
    d = None
    for keep, fresh in terms:
        r = f if x is None else residual(op, f, x)
        step = fresh * (r * op[5])
        d = step if d is None else keep * d + step
        x = d if x is None else x + d
    return x


def split_dot(x, w):
    hi = x.astype(jnp.bfloat16)
    lo = (x - hi.astype(jnp.float32)).astype(jnp.bfloat16)
    return jnp.dot(hi, w, preferred_element_type=jnp.float32) + jnp.dot(
        lo, w, preferred_element_type=jnp.float32
    )


def coarsen(x, tmp, pair):
    rows, cols = x.shape
    if cols % 256:
        x = jnp.concatenate([x, jnp.zeros((rows, 128), jnp.float32)], axis=1)
        cols += 128
    k = cols // 256
    stack = jnp.concatenate([x[:, 256 * j : 256 * j + 256] for j in range(k)], axis=0)
    tmp[: rows * k, :] = split_dot(stack, pair)
    n = rows * k // 2
    s = tmp[pl.ds(0, n, stride=2), :] + tmp[pl.ds(1, n, stride=2), :]
    half = rows // 2
    return [s[half * j : half * (j + 1)] for j in range(k)]


def prolong(x, tmp, pair_t, cols):
    rows = x.shape[0]
    k = x.shape[1] // 128
    for j in range(k):
        tile = x[:, 128 * j : 128 * j + 128]
        tmp[pl.ds(2 * rows * j, rows, stride=2), :] = tile
        tmp[pl.ds(2 * rows * j + 1, rows, stride=2), :] = tile
    out = split_dot(tmp[: 2 * rows * k, :], pair_t)
    out = [out[2 * rows * j : 2 * rows * (j + 1)] for j in range(k)]
    return jnp.concatenate(out, axis=1)[:, :cols]


def kernel(
    plan,
    cond_h, src_h, gnd_h, nod_h, out, cond, nod, gnd, src, in_sem,
    c0, g0, f0, x0, c1, g1, f1, x1, c2, g2, f2, y2, f3, f4, tmp, tmp_up,
    a_row_s, a_row_r, a_col_s, a_col_r, a_cor_s, a_cor_r, a_sem,
    b_row_s, b_row_r, b_cor_s, b_cor_r, b_sem,
    x0_s, x0_r, f1_s, f1_r, x1_s, x1_r, row_sem,
    cg2_g, f2_g, gather_sem,
):
    n_sub, n_blk, halo, widths, coarse_count = plan
    s, b = lax.axis_index("sub"), lax.axis_index("blk")
    w0, w1, w2, w3, w4 = widths
    own = out.shape[1]

    def exists(dr, dc):
        ok = None
        for need, cond_ in (
            (dr < 0, s > 0), (dr > 0, s < n_sub - 1), (dc < 0, b > 0), (dc > 0, b < n_blk - 1),
        ):
            if need:
                ok = cond_ if ok is None else ok & cond_
        return ok

    loads = [
        pltpu.make_async_copy(a, v, in_sem.at[i])
        for i, (a, v) in enumerate(((cond_h, cond), (nod_h, nod), (gnd_h, gnd), (src_h, src)))
    ]
    for load in loads:
        load.start()

    barrier = pltpu.get_barrier_semaphore()
    for dr in range(n_sub):
        @pl.when(s != dr)
        def _():
            pl.semaphore_signal(barrier, 1, device_id={"sub": dr}, device_id_type=MESH)
    for dr, dc in DIRS[2:]:
        @pl.when(exists(dr, dc))
        def _():
            pl.semaphore_signal(
                barrier, 1, device_id={"sub": s + dr, "blk": b + dc}, device_id_type=MESH
            )

    for ref in (c0, g0, f0, c1, g1, f1, y2, f3, f4):
        ref[...] = jnp.zeros_like(ref)

    for load in loads:
        load.wait()
    valid = 1.0 - nod[...].astype(jnp.float32)
    c = cond[...] * valid
    g = gnd[...].astype(jnp.float32) * c
    f = valid * (src[...].astype(jnp.float32) - 0.125)
    c0[4:20, halo : halo + own] = c
    g0[4:20, halo : halo + own] = g
    f0[4:20, halo : halo + own] = f
    for i, (rc, rg) in enumerate(((slice(0, 3), slice(0, 2)), (slice(13, 16), slice(14, 16)))):
        a_row_s[i, 0:3] = c[rc]
        a_row_s[i, 3:5] = g[rg]
        a_row_s[i, 5:7] = f[rg]
        a_row_s[i, 7:8] = jnp.zeros((1, own), jnp.float32)
        for j, lanes in enumerate((slice(0, halo), slice(own - halo, own))):
            a_cor_s[2 * i + j, 0:3] = c[rc, lanes]
            a_cor_s[2 * i + j, 3:5] = g[rg, lanes]
            a_cor_s[2 * i + j, 5:7] = f[rg, lanes]
            a_cor_s[2 * i + j, 7:8] = jnp.zeros((1, halo), jnp.float32)
    for j, lanes in enumerate((slice(0, halo), slice(own - halo, own))):
        a_col_s[j, 0:16] = c[:, lanes]
        a_col_s[j, 16:32] = g[:, lanes]
        a_col_s[j, 32:48] = f[:, lanes]

    has = lambda flag: jnp.where(flag, 1, 0)
    partners = n_sub - 1
    for dr, dc in DIRS[2:]:
        partners = partners + has(exists(dr, dc))
    pl.semaphore_wait(barrier, partners)

    def remote(src_ref, dst_ref, send, recv, dr, dc=0):
        return pltpu.make_async_remote_copy(
            src_ref=src_ref, dst_ref=dst_ref, send_sem=send, recv_sem=recv,
            device_id={"sub": s + dr, "blk": b + dc}, device_id_type=MESH,
        )

    def a_copy(d):
        dr, dc = DIRS[d]
        if d < 2:
            pair_ = a_row_s.at[d], a_row_r.at[d]
        elif d < 4:
            pair_ = a_col_s.at[d - 2], a_col_r.at[d - 2]
        else:
            pair_ = a_cor_s.at[d - 4], a_cor_r.at[d - 4]
        return remote(*pair_, a_sem.at[0, d], a_sem.at[1, d], dr, dc)

    def b_copy(d):
        dr, dc = DIRS[d]
        pair_ = (b_row_s.at[d], b_row_r.at[d]) if d < 2 else (b_cor_s.at[d - 4], b_cor_r.at[d - 4])
        return remote(*pair_, b_sem.at[0, d], b_sem.at[1, d], dr, dc)

    row_bufs = ((x0_s, x0_r), (f1_s, f1_r), (x1_s, x1_r))

    def row_copy(e, d):
        send, recv = row_bufs[e]
        return remote(send.at[d], recv.at[d], row_sem.at[0, e, d], row_sem.at[1, e, d], DIRS[d][0])

    def row_start(e):
        for d in range(2):
            @pl.when(exists(*DIRS[d]))
            def _():
                row_copy(e, d).start()

    def row_wait(e, put):
        for d in range(2):
            @pl.when(exists(-DIRS[d][0], 0))
            def _():
                row_copy(e, d).wait_recv()
                put(d)

    def gather_copy(e, other, sender):
        buf = (cg2_g, f2_g)[e]
        return pltpu.make_async_remote_copy(
            src_ref=buf.at[sender], dst_ref=buf.at[sender],
            send_sem=gather_sem.at[0, e, other], recv_sem=gather_sem.at[1, e, sender],
            device_id={"sub": other}, device_id_type=MESH,
        )

    def gather_start(e):
        for other in range(n_sub):
            @pl.when(s != other)
            def _():
                gather_copy(e, other, s).start()

    def gather_wait(e):
        for other in range(n_sub):
            @pl.when(s != other)
            def _():
                gather_copy(e, other, other).wait_recv()

    for d in range(8):
        @pl.when(exists(*DIRS[d]))
        def _():
            a_copy(d).start()

    iota = lambda shape, dim: lax.broadcasted_iota(jnp.int32, shape, dim)
    pair = jnp.where(
        jnp.right_shift(iota((256, 128), 0), 1) == iota((256, 128), 1), 1.0, 0.0
    ).astype(jnp.bfloat16)
    pair_t = jnp.where(
        jnp.right_shift(iota((128, 256), 1), 1) == iota((128, 256), 0), 1.0, 0.0
    ).astype(jnp.bfloat16)

    h1, own1 = halo // 2, own // 2
    both = jnp.concatenate([0.25 * c, g], axis=0)
    both = jnp.concatenate(coarsen(both, tmp, pair), axis=1)
    c1[4:12, h1 : h1 + own1] = both[0:8]
    g1[4:12, h1 : h1 + own1] = both[8:16]
    for i, (rc, rg) in enumerate(((slice(0, 3), slice(8, 10)), (slice(5, 8), slice(14, 16)))):
        b_row_s[i, 0:3] = both[rc]
        b_row_s[i, 3:5] = both[rg]
        b_row_s[i, 5:8] = jnp.zeros((3, own1), jnp.float32)
        for j, lanes in enumerate((slice(0, h1), slice(own1 - h1, own1))):
            b_cor_s[2 * i + j, 0:3] = both[rc, lanes]
            b_cor_s[2 * i + j, 3:5] = both[rg, lanes]
            b_cor_s[2 * i + j, 5:8] = jnp.zeros((3, h1), jnp.float32)
    for d in (0, 1, 4, 5, 6, 7):
        @pl.when(exists(*DIRS[d]))
        def _():
            b_copy(d).start()

    for d, (dr, dc) in enumerate(DIRS):
        @pl.when(exists(-dr, -dc))
        def _():
            a_copy(d).wait_recv()
            lanes = {0: slice(halo, halo + own), 1: slice(0, halo), -1: slice(halo + own, w0)}[dc]
            if dr == 0:
                for k, ref in enumerate((c0, g0, f0)):
                    ref[4:20, lanes] = a_col_r[d - 2, 16 * k : 16 * k + 16]
            else:
                got = (a_row_r, d) if d < 2 else (a_cor_r, d - 4)
                got = got[0].at[got[1]]
                c0[slice(1, 4) if dr > 0 else slice(20, 23), lanes] = got[0:3]
                near = slice(2, 4) if dr > 0 else slice(20, 22)
                g0[near, lanes] = got[3:5]
                f0[near, lanes] = got[5:7]

    terms = chebyshev_terms(*SMOOTH)
    op0 = level_operator(c0[...], g0[...], False)
    f = f0[...]
    x = smooth(op0, f, None, terms)
    r = residual(op0, f, x)
    rhs = jnp.concatenate(coarsen(r[4:20], tmp, pair), axis=1)
    f1[4:12, :] = rhs
    f1_s[0] = rhs[0:2]
    f1_s[1] = rhs[6:8]
    row_start(1)
    x0[...] = x
    x0_s[0] = x[4:6]
    x0_s[1] = x[18:20]
    row_start(0)

    sides = (slice(0, halo), slice(halo + own, w0))
    both = jnp.concatenate(
        [jnp.concatenate([0.25 * c0[4:20, v], g0[4:20, v]], axis=0) for v in sides], axis=1
    )
    both = jnp.concatenate(coarsen(both, tmp, pair), axis=1)
    for k, lanes in enumerate((slice(0, h1), slice(h1 + own1, 2 * h1 + own1))):
        c1[4:12, lanes] = both[0:8, h1 * k : h1 * k + h1]
        g1[4:12, lanes] = both[8:16, h1 * k : h1 * k + h1]
    both = jnp.concatenate([0.25 * c1[4:12, :], g1[4:12, :]], axis=0)
    cg2_g[s] = jnp.concatenate(coarsen(both, tmp, pair), axis=1)
    gather_start(0)
    for d in (0, 1, 4, 5, 6, 7):
        dr, dc = DIRS[d]
        @pl.when(exists(-dr, -dc))
        def _():
            b_copy(d).wait_recv()
            lanes = {0: slice(h1, h1 + own1), 1: slice(0, h1), -1: slice(h1 + own1, w1)}[dc]
            got = b_row_r.at[d] if d < 2 else b_cor_r.at[d - 4]
            c1[slice(1, 4) if dr > 0 else slice(12, 15), lanes] = got[0:3]
            g1[slice(2, 4) if dr > 0 else slice(12, 14), lanes] = got[3:5]
    op1 = level_operator(c1[...], g1[...], False)

    def put_f1(d):
        f1[slice(12, 14) if d == 0 else slice(2, 4), :] = f1_r[d]

    row_wait(1, put_f1)
    fl1 = f1[...]
    x = smooth(op1, fl1, None, terms)
    r = residual(op1, fl1, x)
    f2_g[s] = jnp.concatenate(coarsen(r[4:12], tmp, pair), axis=1)
    gather_start(1)
    x1[...] = x
    x1_s[0] = x[4:7]
    x1_s[1] = x[9:12]
    row_start(2)

    gather_wait(0)
    for k in range(n_sub):
        c2[4 * k : 4 * k + 4, :] = cg2_g[k, 0:4]
        g2[4 * k : 4 * k + 4, :] = cg2_g[k, 4:8]

    cg = (c2[...], g2[...])
    ops = [level_operator(*cg, True)]
    rows = 4 * n_sub
    for level, width in ((3, w3), (4, w4)):
        rows //= 2
        full = max(rows, 8)
        parts = []
        for k, v in enumerate(cg):
            tiles = coarsen(0.25 * v if k == 0 else v, tmp, pair)
            v = jnp.concatenate(tiles, axis=1)[:rows]
            if full > rows:
                v = jnp.concatenate([v, jnp.zeros((full - rows, width), jnp.float32)], axis=0)
            parts.append(v)
        cg = tuple(parts)
        ops.append(level_operator(*cg, True))

    gather_wait(1)
    for k in range(n_sub):
        f2[4 * k : 4 * k + 4, :] = f2_g[k]
    rhs = f2[...]
    kept = []
    rows = 4 * n_sub
    for level in (2, 3):
        op = ops[level - 2]
        x = smooth(op, rhs, None, terms)
        r = residual(op, rhs, x)
        kept.append((rhs, x))
        rows //= 2
        ref = (f3, f4)[level - 2]
        for j, tile in enumerate(coarsen(r, tmp, pair)):
            ref[:rows, 128 * j : 128 * j + 128] = tile
        rhs = ref[...]
    y = smooth(ops[2], rhs, None, chebyshev_terms(coarse_count, COARSE_LOW, COARSE_HIGH))
    for level, width in ((3, w3), (2, w2)):
        op = ops[level - 2]
        rhs, x = kept[level - 2]
        rows = n_sub if level == 3 else 2 * n_sub
        y = x + op[6] * prolong(y[:rows], tmp_up, pair_t, width)
        y = smooth(op, rhs, y, terms)

    for k in range(n_sub):
        y2[k + 1] = y[4 * k : 4 * k + 4]
    y = jnp.concatenate([y2[s][2:4], y2[s + 1], y2[s + 2][0:2]], axis=0)

    def put_x1(d):
        x1[slice(12, 15) if d == 0 else slice(1, 4), :] = x1_r[d]

    row_wait(2, put_x1)
    y = x1[...] + op1[6] * prolong(y, tmp_up, pair_t, w1)
    y = smooth(op1, fl1, y, terms)

    def put_x0(d):
        x0[slice(20, 22) if d == 0 else slice(2, 4), :] = x0_r[d]

    row_wait(0, put_x0)
    y = x0[...] + op0[6] * prolong(y[2:14], tmp_up, pair_t, w0)
    y = smooth(op0, f0[...], y, terms)
    out[...] = y[4:20, halo : halo + own]

    for d in range(8):
        @pl.when(exists(*DIRS[d]))
        def _():
            a_copy(d).wait_send()
    for d in (0, 1, 4, 5, 6, 7):
        @pl.when(exists(*DIRS[d]))
        def _():
            b_copy(d).wait_send()
    for e in range(3):
        for d in range(2):
            @pl.when(exists(*DIRS[d]))
            def _():
                row_copy(e, d).wait_send()
    for e in range(2):
        for other in range(n_sub):
            @pl.when(s != other)
            def _():
                gather_copy(e, other, s).wait_send()


def body(conductance, source_mask, ground_mask, nodata_mask):
    n_sub, n_blk = lax.axis_size("sub"), lax.axis_size("blk")
    rows, own = conductance.shape
    assert rows == 16 and own % 256 == 0
    coarse_count = 8 + n_sub // 2
    need = coarse_count + 2
    for _ in range(LEVELS - 1):
        need = 2 * need + 2
    halo = round_up(need, 256)
    assert halo <= own
    w0 = own + 2 * halo
    widths = (w0,) + tuple(round_up(w0 >> l, 128) for l in range(1, 5))
    w1, w2, w3, w4 = widths[1:]
    f32 = lambda *shape: pltpu.VMEM(shape, jnp.float32)
    i32 = lambda *shape: pltpu.VMEM(shape, jnp.int32)
    sem = lambda *shape: pltpu.SemaphoreType.DMA(shape)
    r2, r3, r4 = 4 * n_sub, max(2 * n_sub, 8), max(n_sub, 8)
    tmp_rows = max(32 * round_up(w0, 256) // 256, 4 * n_sub * round_up(w2, 256) // 256)
    up_rows = max(24 * w1 // 128, 4 * n_sub * w3 // 128)
    vmem = pl.BlockSpec(memory_space=pltpu.VMEM)
    return pl.pallas_call(
        functools.partial(kernel, (n_sub, n_blk, halo, widths, coarse_count)),
        out_shape=jax.ShapeDtypeStruct((rows, own), jnp.float32),
        in_specs=[pl.BlockSpec(memory_space=pltpu.HBM)] * 4,
        out_specs=vmem,
        scratch_shapes=[
            f32(rows, own), i32(rows, own), i32(rows, own), i32(rows, own), sem(4),
            f32(24, w0), f32(24, w0), f32(24, w0), f32(24, w0),
            f32(16, w1), f32(16, w1), f32(16, w1), f32(16, w1),
            f32(r2, w2), f32(r2, w2), f32(r2, w2), f32(n_sub + 2, 4, w2),
            f32(r3, w3), f32(r4, w4), f32(tmp_rows, 128), f32(up_rows, 128),
            f32(2, 8, own), f32(2, 8, own), f32(2, 48, halo), f32(2, 48, halo),
            f32(4, 8, halo), f32(4, 8, halo), sem(2, 8),
            f32(2, 8, own // 2), f32(2, 8, own // 2), f32(4, 8, halo // 2), f32(4, 8, halo // 2), sem(2, 8),
            f32(2, 2, w0), f32(2, 2, w0),
            f32(2, 2, w1), f32(2, 2, w1), f32(2, 3, w1), f32(2, 3, w1), sem(2, 3, 2),
            f32(n_sub, 8, w2), f32(n_sub, 4, w2), sem(2, 2, n_sub),
        ],
        compiler_params=pltpu.CompilerParams(
            collective_id=0, has_side_effects=True, vmem_limit_bytes=40 * 1024 * 1024
        ),
    )(conductance, source_mask, ground_mask, nodata_mask)


def solution(mesh):
    spec = P(("groups", "sub"), "blk")
    return jax.shard_map(
        body, mesh=mesh, in_specs=(spec,) * 4, out_specs=spec, check_vma=False
    )
```

```python
import functools
import jax
import jax.numpy as jnp
from jax import lax
from jax.experimental import pallas as pl
from jax.experimental.pallas import tpu as pltpu
from jax.sharding import PartitionSpec as P

LEVELS = 5
SMOOTH = (2, 0.5, 2.0)
COARSE_LOW, COARSE_HIGH = 0.02, 2.0
DIRS = ((-1, 0), (1, 0), (0, -1), (0, 1), (-1, -1), (-1, 1), (1, -1), (1, 1))
MESH = pl.DeviceIdType.MESH


def round_up(n, k):
    return -(-n // k) * k


def chebyshev_terms(sweep_count, low_end, high_end):
    mid = 0.5 * (high_end + low_end)
    half = 0.5 * (high_end - low_end)
    sigma = mid / half
    rho = 1.0 / sigma
    terms = [(0.0, 1.0 / mid)]
    for _ in range(1, sweep_count):
        rho_next = 1.0 / (2.0 * sigma - rho)
        terms.append((rho_next * rho, 2.0 * rho_next / half))
        rho = rho_next
    return terms


def rolled(x, shift, axis):
    return pltpu.roll(x, shift % x.shape[axis], axis)


def level_operator(c, g, whole_rows):
    rows, cols = c.shape
    h = 0.5 * c
    valid = c > 0.0
    c_r = rolled(c, -1, 1)
    c_d = rolled(c, -1, 0)
    e_r = jnp.where(valid & (c_r > 0.0), h + 0.5 * c_r, 0.0)
    ok_d = valid & (c_d > 0.0)
    if whole_rows:
        ok_d = ok_d & (lax.broadcasted_iota(jnp.int32, c.shape, 0) < rows - 1)
    e_d = jnp.where(ok_d, h + 0.5 * c_d, 0.0)
    e_l = rolled(e_r, 1, 1)
    e_u = rolled(e_d, 1, 0)
    m = jnp.where(valid, 1.0, 0.0)
    diag = e_d + e_u + e_r + e_l + g + (1.0 - m)
    inv = 1.0 / jnp.maximum(diag, 0.25 * c)
    return e_r, e_l, e_d, e_u, diag, inv, m


def residual(op, f, x):
    e_r, e_l, e_d, e_u, diag, inv, m = op
    out = f - diag * x
    out = out + e_r * rolled(x, -1, 1) + e_l * rolled(x, 1, 1)
    return out + e_d * rolled(x, -1, 0) + e_u * rolled(x, 1, 0)


def smooth(op, f, x, terms):
    d = None
    for keep, fresh in terms:
        r = f if x is None else residual(op, f, x)
        step = fresh * (r * op[5])
        d = step if d is None else keep * d + step
        x = d if x is None else x + d
    return x


def split_dot(x, w):
    hi = x.astype(jnp.bfloat16)
    lo = (x - hi.astype(jnp.float32)).astype(jnp.bfloat16)
    return jnp.dot(hi, w, preferred_element_type=jnp.float32) + jnp.dot(
        lo, w, preferred_element_type=jnp.float32
    )


def coarsen(x, tmp, pair):
    rows, cols = x.shape
    if cols % 256:
        x = jnp.concatenate([x, jnp.zeros((rows, 128), jnp.float32)], axis=1)
        cols += 128
    k = cols // 256
    stack = jnp.concatenate([x[:, 256 * j : 256 * j + 256] for j in range(k)], axis=0)
    tmp[: rows * k, :] = split_dot(stack, pair)
    n = rows * k // 2
    s = tmp[pl.ds(0, n, stride=2), :] + tmp[pl.ds(1, n, stride=2), :]
    half = rows // 2
    return [s[half * j : half * (j + 1)] for j in range(k)]


def prolong(x, tmp, pair_t, cols):
    rows = x.shape[0]
    k = x.shape[1] // 128
    for j in range(k):
        tile = x[:, 128 * j : 128 * j + 128]
        tmp[pl.ds(2 * rows * j, rows, stride=2), :] = tile
        tmp[pl.ds(2 * rows * j + 1, rows, stride=2), :] = tile
    out = split_dot(tmp[: 2 * rows * k, :], pair_t)
    out = [out[2 * rows * j : 2 * rows * (j + 1)] for j in range(k)]
    return jnp.concatenate(out, axis=1)[:, :cols]


def kernel(
    plan,
    cond_h, src_h, gnd_h, nod_h, out, cond, nod, gnd, src, in_sem,
    c0, g0, f0, x0, c1, g1, f1, x1, c2, g2, f2, y2, f3, f4, tmp, tmp_up,
    a_row_s, a_row_r, a_col_s, a_col_r, a_cor_s, a_cor_r, a_sem,
    b_row_s, b_row_r, b_cor_s, b_cor_r, b_sem,
    x0_s, x0_r, f1_s, f1_r, x1_s, x1_r, row_sem,
    cg2_g, f2_g, gather_sem,
):
    n_sub, n_blk, halo, widths, coarse_count = plan
    s, b = lax.axis_index("sub"), lax.axis_index("blk")
    w0, w1, w2, w3, w4 = widths
    own = out.shape[1]

    def exists(dr, dc):
        ok = None
        for need, cond_ in (
            (dr < 0, s > 0), (dr > 0, s < n_sub - 1), (dc < 0, b > 0), (dc > 0, b < n_blk - 1),
        ):
            if need:
                ok = cond_ if ok is None else ok & cond_
        return ok

    loads = [
        pltpu.make_async_copy(a, v, in_sem.at[i])
        for i, (a, v) in enumerate(((cond_h, cond), (nod_h, nod), (gnd_h, gnd), (src_h, src)))
    ]
    for load in loads:
        load.start()

    barrier = pltpu.get_barrier_semaphore()
    for dr in range(n_sub):
        @pl.when(s != dr)
        def _():
            pl.semaphore_signal(barrier, 1, device_id={"sub": dr}, device_id_type=MESH)
    for dr, dc in DIRS[2:]:
        @pl.when(exists(dr, dc))
        def _():
            pl.semaphore_signal(
                barrier, 1, device_id={"sub": s + dr, "blk": b + dc}, device_id_type=MESH
            )

    for ref in (c0, g0, f0, c1, g1, f1, y2, f3, f4):
        ref[...] = jnp.zeros_like(ref)

    for load in loads:
        load.wait()
    valid = 1.0 - nod[...].astype(jnp.float32)
    c = cond[...] * valid
    g = gnd[...].astype(jnp.float32) * c
    f = valid * (src[...].astype(jnp.float32) - 0.125)
    c0[4:20, halo : halo + own] = c
    g0[4:20, halo : halo + own] = g
    f0[4:20, halo : halo + own] = f
    for i, (rc, rg) in enumerate(((slice(0, 3), slice(0, 2)), (slice(13, 16), slice(14, 16)))):
        a_row_s[i, 0:3] = c[rc]
        a_row_s[i, 3:5] = g[rg]
        a_row_s[i, 5:7] = f[rg]
        a_row_s[i, 7:8] = jnp.zeros((1, own), jnp.float32)
        for j, lanes in enumerate((slice(0, halo), slice(own - halo, own))):
            a_cor_s[2 * i + j, 0:3] = c[rc, lanes]
            a_cor_s[2 * i + j, 3:5] = g[rg, lanes]
            a_cor_s[2 * i + j, 5:7] = f[rg, lanes]
            a_cor_s[2 * i + j, 7:8] = jnp.zeros((1, halo), jnp.float32)
    for j, lanes in enumerate((slice(0, halo), slice(own - halo, own))):
        a_col_s[j, 0:16] = c[:, lanes]
        a_col_s[j, 16:32] = g[:, lanes]
        a_col_s[j, 32:48] = f[:, lanes]

    has = lambda flag: jnp.where(flag, 1, 0)
    partners = n_sub - 1
    for dr, dc in DIRS[2:]:
        partners = partners + has(exists(dr, dc))
    pl.semaphore_wait(barrier, partners)

    def remote(src_ref, dst_ref, send, recv, dr, dc=0):
        return pltpu.make_async_remote_copy(
            src_ref=src_ref, dst_ref=dst_ref, send_sem=send, recv_sem=recv,
            device_id={"sub": s + dr, "blk": b + dc}, device_id_type=MESH,
        )

    def a_copy(d):
        dr, dc = DIRS[d]
        if d < 2:
            pair_ = a_row_s.at[d], a_row_r.at[d]
        elif d < 4:
            pair_ = a_col_s.at[d - 2], a_col_r.at[d - 2]
        else:
            pair_ = a_cor_s.at[d - 4], a_cor_r.at[d - 4]
        return remote(*pair_, a_sem.at[0, d], a_sem.at[1, d], dr, dc)

    def b_copy(d):
        dr, dc = DIRS[d]
        pair_ = (b_row_s.at[d], b_row_r.at[d]) if d < 2 else (b_cor_s.at[d - 4], b_cor_r.at[d - 4])
        return remote(*pair_, b_sem.at[0, d], b_sem.at[1, d], dr, dc)

    row_bufs = ((x0_s, x0_r), (f1_s, f1_r), (x1_s, x1_r))

    def row_copy(e, d):
        send, recv = row_bufs[e]
        return remote(send.at[d], recv.at[d], row_sem.at[0, e, d], row_sem.at[1, e, d], DIRS[d][0])

    def row_start(e):
        for d in range(2):
            @pl.when(exists(*DIRS[d]))
            def _():
                row_copy(e, d).start()

    def row_wait(e, put):
        for d in range(2):
            @pl.when(exists(-DIRS[d][0], 0))
            def _():
                row_copy(e, d).wait_recv()
                put(d)

    def gather_copy(e, other, sender):
        buf = (cg2_g, f2_g)[e]
        return pltpu.make_async_remote_copy(
            src_ref=buf.at[sender], dst_ref=buf.at[sender],
            send_sem=gather_sem.at[0, e, other], recv_sem=gather_sem.at[1, e, sender],
            device_id={"sub": other}, device_id_type=MESH,
        )

    def gather_start(e):
        for other in range(n_sub):
            @pl.when(s != other)
            def _():
                gather_copy(e, other, s).start()

    def gather_wait(e):
        for other in range(n_sub):
            @pl.when(s != other)
            def _():
                gather_copy(e, other, other).wait_recv()

    for d in range(8):
        @pl.when(exists(*DIRS[d]))
        def _():
            a_copy(d).start()

    iota = lambda shape, dim: lax.broadcasted_iota(jnp.int32, shape, dim)
    pair = jnp.where(
        jnp.right_shift(iota((256, 128), 0), 1) == iota((256, 128), 1), 1.0, 0.0
    ).astype(jnp.bfloat16)
    pair_t = jnp.where(
        jnp.right_shift(iota((128, 256), 1), 1) == iota((128, 256), 0), 1.0, 0.0
    ).astype(jnp.bfloat16)

    h1, own1 = halo // 2, own // 2
    both = jnp.concatenate([0.25 * c, g], axis=0)
    both = jnp.concatenate(coarsen(both, tmp, pair), axis=1)
    c1[4:12, h1 : h1 + own1] = both[0:8]
    g1[4:12, h1 : h1 + own1] = both[8:16]
    for i, (rc, rg) in enumerate(((slice(0, 3), slice(8, 10)), (slice(5, 8), slice(14, 16)))):
        b_row_s[i, 0:3] = both[rc]
        b_row_s[i, 3:5] = both[rg]
        b_row_s[i, 5:8] = jnp.zeros((3, own1), jnp.float32)
        for j, lanes in enumerate((slice(0, h1), slice(own1 - h1, own1))):
            b_cor_s[2 * i + j, 0:3] = both[rc, lanes]
            b_cor_s[2 * i + j, 3:5] = both[rg, lanes]
            b_cor_s[2 * i + j, 5:8] = jnp.zeros((3, h1), jnp.float32)
    for d in (0, 1, 4, 5, 6, 7):
        @pl.when(exists(*DIRS[d]))
        def _():
            b_copy(d).start()

    for d, (dr, dc) in enumerate(DIRS):
        @pl.when(exists(-dr, -dc))
        def _():
            a_copy(d).wait_recv()
            lanes = {0: slice(halo, halo + own), 1: slice(0, halo), -1: slice(halo + own, w0)}[dc]
            if dr == 0:
                for k, ref in enumerate((c0, g0, f0)):
                    ref[4:20, lanes] = a_col_r[d - 2, 16 * k : 16 * k + 16]
            else:
                got = (a_row_r, d) if d < 2 else (a_cor_r, d - 4)
                got = got[0].at[got[1]]
                c0[slice(1, 4) if dr > 0 else slice(20, 23), lanes] = got[0:3]
                near = slice(2, 4) if dr > 0 else slice(20, 22)
                g0[near, lanes] = got[3:5]
                f0[near, lanes] = got[5:7]

    terms = chebyshev_terms(*SMOOTH)
    op0 = level_operator(c0[...], g0[...], False)
    f = f0[...]
    x = smooth(op0, f, None, terms)
    r = residual(op0, f, x)
    rhs = jnp.concatenate(coarsen(r[4:20], tmp, pair), axis=1)
    f1[4:12, :] = rhs
    f1_s[0] = rhs[0:2]
    f1_s[1] = rhs[6:8]
    row_start(1)
    x0[...] = x
    x0_s[0] = x[4:6]
    x0_s[1] = x[18:20]
    row_start(0)

    sides = (slice(0, halo), slice(halo + own, w0))
    both = jnp.concatenate(
        [jnp.concatenate([0.25 * c0[4:20, v], g0[4:20, v]], axis=0) for v in sides], axis=1
    )
    both = jnp.concatenate(coarsen(both, tmp, pair), axis=1)
    for k, lanes in enumerate((slice(0, h1), slice(h1 + own1, 2 * h1 + own1))):
        c1[4:12, lanes] = both[0:8, h1 * k : h1 * k + h1]
        g1[4:12, lanes] = both[8:16, h1 * k : h1 * k + h1]
    both = jnp.concatenate([0.25 * c1[4:12, :], g1[4:12, :]], axis=0)
    cg2_g[s] = jnp.concatenate(coarsen(both, tmp, pair), axis=1)
    gather_start(0)
    for d in (0, 1, 4, 5, 6, 7):
        dr, dc = DIRS[d]
        @pl.when(exists(-dr, -dc))
        def _():
            b_copy(d).wait_recv()
            lanes = {0: slice(h1, h1 + own1), 1: slice(0, h1), -1: slice(h1 + own1, w1)}[dc]
            got = b_row_r.at[d] if d < 2 else b_cor_r.at[d - 4]
            c1[slice(1, 4) if dr > 0 else slice(12, 15), lanes] = got[0:3]
            g1[slice(2, 4) if dr > 0 else slice(12, 14), lanes] = got[3:5]
    op1 = level_operator(c1[...], g1[...], False)

    def put_f1(d):
        f1[slice(12, 14) if d == 0 else slice(2, 4), :] = f1_r[d]

    row_wait(1, put_f1)
    fl1 = f1[...]
    x = smooth(op1, fl1, None, terms)
    r = residual(op1, fl1, x)
    f2_g[s] = jnp.concatenate(coarsen(r[4:12], tmp, pair), axis=1)
    gather_start(1)
    x1[...] = x
    x1_s[0] = x[4:7]
    x1_s[1] = x[9:12]
    row_start(2)

    gather_wait(0)
    for k in range(n_sub):
        c2[4 * k : 4 * k + 4, :] = cg2_g[k, 0:4]
        g2[4 * k : 4 * k + 4, :] = cg2_g[k, 4:8]

    cg = (c2[...], g2[...])
    ops = [level_operator(*cg, True)]
    rows = 4 * n_sub
    for level, width in ((3, w3), (4, w4)):
        rows //= 2
        full = max(rows, 8)
        parts = []
        for k, v in enumerate(cg):
            tiles = coarsen(0.25 * v if k == 0 else v, tmp, pair)
            v = jnp.concatenate(tiles, axis=1)[:rows]
            if full > rows:
                v = jnp.concatenate([v, jnp.zeros((full - rows, width), jnp.float32)], axis=0)
            parts.append(v)
        cg = tuple(parts)
        ops.append(level_operator(*cg, True))

    gather_wait(1)
    for k in range(n_sub):
        f2[4 * k : 4 * k + 4, :] = f2_g[k]
    rhs = f2[...]
    kept = []
    rows = 4 * n_sub
    for level in (2, 3):
        op = ops[level - 2]
        x = smooth(op, rhs, None, terms)
        r = residual(op, rhs, x)
        kept.append((rhs, x))
        rows //= 2
        ref = (f3, f4)[level - 2]
        for j, tile in enumerate(coarsen(r, tmp, pair)):
            ref[:rows, 128 * j : 128 * j + 128] = tile
        rhs = ref[...]
    y = smooth(ops[2], rhs, None, chebyshev_terms(coarse_count, COARSE_LOW, COARSE_HIGH))
    for level, width in ((3, w3), (2, w2)):
        op = ops[level - 2]
        rhs, x = kept[level - 2]
        rows = n_sub if level == 3 else 2 * n_sub
        y = x + op[6] * prolong(y[:rows], tmp_up, pair_t, width)
        y = smooth(op, rhs, y, terms)

    for k in range(n_sub):
        y2[k + 1] = y[4 * k : 4 * k + 4]
    y = jnp.concatenate([y2[s][2:4], y2[s + 1], y2[s + 2][0:2]], axis=0)

    def put_x1(d):
        x1[slice(12, 15) if d == 0 else slice(1, 4), :] = x1_r[d]

    row_wait(2, put_x1)
    y = x1[...] + op1[6] * prolong(y, tmp_up, pair_t, w1)
    y = smooth(op1, fl1, y, terms)

    def put_x0(d):
        x0[slice(20, 22) if d == 0 else slice(2, 4), :] = x0_r[d]

    row_wait(0, put_x0)
    y = x0[...] + op0[6] * prolong(y[2:14], tmp_up, pair_t, w0)
    y = smooth(op0, f0[...], y, terms)
    out[...] = y[4:20, halo : halo + own]

    for d in range(8):
        @pl.when(exists(*DIRS[d]))
        def _():
            a_copy(d).wait_send()
    for d in (0, 1, 4, 5, 6, 7):
        @pl.when(exists(*DIRS[d]))
        def _():
            b_copy(d).wait_send()
    for e in range(3):
        for d in range(2):
            @pl.when(exists(*DIRS[d]))
            def _():
                row_copy(e, d).wait_send()
    for e in range(2):
        for other in range(n_sub):
            @pl.when(s != other)
            def _():
                gather_copy(e, other, s).wait_send()


def body(conductance, source_mask, ground_mask, nodata_mask):
    n_sub, n_blk = lax.axis_size("sub"), lax.axis_size("blk")
    rows, own = conductance.shape
    assert rows == 16 and own % 256 == 0
    coarse_count = 8 + n_sub // 2
    need = coarse_count + 2
    for _ in range(LEVELS - 1):
        need = 2 * need + 2
    halo = round_up(need, 256)
    assert halo <= own
    w0 = own + 2 * halo
    widths = (w0,) + tuple(round_up(w0 >> l, 128) for l in range(1, 5))
    w1, w2, w3, w4 = widths[1:]
    f32 = lambda *shape: pltpu.VMEM(shape, jnp.float32)
    i32 = lambda *shape: pltpu.VMEM(shape, jnp.int32)
    sem = lambda *shape: pltpu.SemaphoreType.DMA(shape)
    r2, r3, r4 = 4 * n_sub, max(2 * n_sub, 8), max(n_sub, 8)
    tmp_rows = max(32 * round_up(w0, 256) // 256, 4 * n_sub * round_up(w2, 256) // 256)
    up_rows = max(24 * w1 // 128, 4 * n_sub * w3 // 128)
    vmem = pl.BlockSpec(memory_space=pltpu.VMEM)
    args = (conductance, source_mask, ground_mask, nodata_mask)
    args = [pltpu.with_memory_space_constraint(v, pltpu.HBM) for v in args]
    return pl.pallas_call(
        functools.partial(kernel, (n_sub, n_blk, halo, widths, coarse_count)),
        out_shape=jax.ShapeDtypeStruct((rows, own), jnp.float32),
        in_specs=[pl.BlockSpec(memory_space=pltpu.HBM)] * 4,
        out_specs=vmem,
        scratch_shapes=[
            f32(rows, own), i32(rows, own), i32(rows, own), i32(rows, own), sem(4),
            f32(24, w0), f32(24, w0), f32(24, w0), f32(24, w0),
            f32(16, w1), f32(16, w1), f32(16, w1), f32(16, w1),
            f32(r2, w2), f32(r2, w2), f32(r2, w2), f32(n_sub + 2, 4, w2),
            f32(r3, w3), f32(r4, w4), f32(tmp_rows, 128), f32(up_rows, 128),
            f32(2, 8, own), f32(2, 8, own), f32(2, 48, halo), f32(2, 48, halo),
            f32(4, 8, halo), f32(4, 8, halo), sem(2, 8),
            f32(2, 8, own // 2), f32(2, 8, own // 2), f32(4, 8, halo // 2), f32(4, 8, halo // 2), sem(2, 8),
            f32(2, 2, w0), f32(2, 2, w0),
            f32(2, 2, w1), f32(2, 2, w1), f32(2, 3, w1), f32(2, 3, w1), sem(2, 3, 2),
            f32(n_sub, 8, w2), f32(n_sub, 4, w2), sem(2, 2, n_sub),
        ],
        compiler_params=pltpu.CompilerParams(
            collective_id=0, has_side_effects=True, vmem_limit_bytes=40 * 1024 * 1024
        ),
    )(*args)


def solution(mesh):
    spec = P(("groups", "sub"), "blk")
    return jax.shard_map(
        body, mesh=mesh, in_specs=(spec,) * 4, out_specs=spec, check_vma=False
    )
```

```python
import functools
import jax
import jax.numpy as jnp
from jax import lax
from jax.experimental import pallas as pl
from jax.experimental.pallas import tpu as pltpu
from jax.sharding import PartitionSpec as P

LEVELS = 5
SMOOTH = (2, 0.5, 2.0)
COARSE_LOW, COARSE_HIGH = 0.02, 2.0
DIRS = ((-1, 0), (1, 0), (0, -1), (0, 1), (-1, -1), (-1, 1), (1, -1), (1, 1))
MESH = pl.DeviceIdType.MESH


def round_up(n, k):
    return -(-n // k) * k


def chebyshev_terms(sweep_count, low_end, high_end):
    mid = 0.5 * (high_end + low_end)
    half = 0.5 * (high_end - low_end)
    sigma = mid / half
    rho = 1.0 / sigma
    terms = [(0.0, 1.0 / mid)]
    for _ in range(1, sweep_count):
        rho_next = 1.0 / (2.0 * sigma - rho)
        terms.append((rho_next * rho, 2.0 * rho_next / half))
        rho = rho_next
    return terms


def rolled(x, shift, axis):
    return pltpu.roll(x, shift % x.shape[axis], axis)


def level_operator(c, g, whole_rows):
    rows, cols = c.shape
    h = 0.5 * c
    valid = c > 0.0
    c_r = rolled(c, -1, 1)
    c_d = rolled(c, -1, 0)
    e_r = jnp.where(valid & (c_r > 0.0), h + 0.5 * c_r, 0.0)
    ok_d = valid & (c_d > 0.0)
    if whole_rows:
        ok_d = ok_d & (lax.broadcasted_iota(jnp.int32, c.shape, 0) < rows - 1)
    e_d = jnp.where(ok_d, h + 0.5 * c_d, 0.0)
    e_l = rolled(e_r, 1, 1)
    e_u = rolled(e_d, 1, 0)
    m = jnp.where(valid, 1.0, 0.0)
    diag = e_d + e_u + e_r + e_l + g + (1.0 - m)
    inv = 1.0 / jnp.maximum(diag, 0.25 * c)
    return e_r, e_l, e_d, e_u, diag, inv, m


def residual(op, f, x):
    e_r, e_l, e_d, e_u, diag, inv, m = op
    out = f - diag * x
    out = out + e_r * rolled(x, -1, 1) + e_l * rolled(x, 1, 1)
    return out + e_d * rolled(x, -1, 0) + e_u * rolled(x, 1, 0)


def smooth(op, f, x, terms):
    d = None
    for keep, fresh in terms:
        r = f if x is None else residual(op, f, x)
        step = fresh * (r * op[5])
        d = step if d is None else keep * d + step
        x = d if x is None else x + d
    return x


def lane_take(x, which):
    lane = lax.broadcasted_iota(jnp.int32, x.shape, 1)
    if which == 0:
        index = jnp.bitwise_and(2 * lane, 127)
    else:
        index = jnp.right_shift(lane, 1) + 64 * (which - 1)
    return jnp.take_along_axis(x, index, axis=1, mode="promise_in_bounds")


def coarsen(x, tmp):
    rows, cols = x.shape
    k = round_up(cols, 256) // 256
    half = rows // 2
    sums = []
    for odd in range(2):
        base = odd * rows * k
        for j in range(k):
            lanes = 256 * j + 128 * odd
            if lanes < cols:
                tile = x[:, lanes : lanes + 128]
            else:
                tile = jnp.zeros((rows, 128), jnp.float32)
            tmp[base + rows * j : base + rows * (j + 1), :] = tile
        t = tmp[pl.ds(base, half * k, stride=2), :] + tmp[pl.ds(base + 1, half * k, stride=2), :]
        sums.append(lane_take(t + rolled(t, -1, 1), 0))
    lane = lax.broadcasted_iota(jnp.int32, sums[0].shape, 1)
    s = jnp.where(lane < 64, *sums)
    return [s[half * j : half * (j + 1)] for j in range(k)]


def prolong(x, first, rows, tmp, cols):
    n = cols // 128
    for j in range(x.shape[1] // 128):
        tile = x[:, 128 * j : 128 * j + 128]
        for side in range(2):
            if 2 * j + side < n:
                base = 2 * rows * (2 * j + side)
                v = lane_take(tile, 1 + side)[first : first + rows]
                tmp[pl.ds(base, rows, stride=2), :] = v
                tmp[pl.ds(base + 1, rows, stride=2), :] = v
    return jnp.concatenate([tmp[2 * rows * j : 2 * rows * (j + 1), :] for j in range(n)], axis=1)


def kernel(
    plan,
    cond_h, src_h, gnd_h, nod_h, out, cond, nod, gnd, src, in_sem,
    c0, g0, f0, x0, c1, g1, f1, x1, c2, g2, f2, y2, f3, f4, tmp, tmp_up,
    a_row_s, a_row_r, a_col_s, a_col_r, a_cor_s, a_cor_r, a_sem,
    b_row_s, b_row_r, b_cor_s, b_cor_r, b_sem,
    x0_s, x0_r, f1_s, f1_r, x1_s, x1_r, row_sem,
    cg2_g, f2_g, gather_sem,
):
    n_sub, n_blk, halo, widths, coarse_count = plan
    s, b = lax.axis_index("sub"), lax.axis_index("blk")
    w0, w1, w2, w3, w4 = widths
    own = out.shape[1]

    def exists(dr, dc):
        ok = None
        for need, cond_ in (
            (dr < 0, s > 0), (dr > 0, s < n_sub - 1), (dc < 0, b > 0), (dc > 0, b < n_blk - 1),
        ):
            if need:
                ok = cond_ if ok is None else ok & cond_
        return ok

    loads = [
        pltpu.make_async_copy(a, v, in_sem.at[i])
        for i, (a, v) in enumerate(((cond_h, cond), (nod_h, nod), (gnd_h, gnd), (src_h, src)))
    ]
    for load in loads:
        load.start()

    barrier = pltpu.get_barrier_semaphore()
    for dr in range(n_sub):
        @pl.when(s != dr)
        def _():
            pl.semaphore_signal(barrier, 1, device_id={"sub": dr}, device_id_type=MESH)
    for dr, dc in DIRS[2:]:
        @pl.when(exists(dr, dc))
        def _():
            pl.semaphore_signal(
                barrier, 1, device_id={"sub": s + dr, "blk": b + dc}, device_id_type=MESH
            )

    for ref in (c0, g0, f0, c1, g1, f1, y2, f3, f4):
        ref[...] = jnp.zeros_like(ref)

    for load in loads:
        load.wait()
    valid = 1.0 - nod[...].astype(jnp.float32)
    c = cond[...] * valid
    g = gnd[...].astype(jnp.float32) * c
    f = valid * (src[...].astype(jnp.float32) - 0.125)
    c0[4:20, halo : halo + own] = c
    g0[4:20, halo : halo + own] = g
    f0[4:20, halo : halo + own] = f
    for i, (rc, rg) in enumerate(((slice(0, 3), slice(0, 2)), (slice(13, 16), slice(14, 16)))):
        a_row_s[i, 0:3] = c[rc]
        a_row_s[i, 3:5] = g[rg]
        a_row_s[i, 5:7] = f[rg]
        a_row_s[i, 7:8] = jnp.zeros((1, own), jnp.float32)
        for j, lanes in enumerate((slice(0, halo), slice(own - halo, own))):
            a_cor_s[2 * i + j, 0:3] = c[rc, lanes]
            a_cor_s[2 * i + j, 3:5] = g[rg, lanes]
            a_cor_s[2 * i + j, 5:7] = f[rg, lanes]
            a_cor_s[2 * i + j, 7:8] = jnp.zeros((1, halo), jnp.float32)
    for j, lanes in enumerate((slice(0, halo), slice(own - halo, own))):
        a_col_s[j, 0:16] = c[:, lanes]
        a_col_s[j, 16:32] = g[:, lanes]
        a_col_s[j, 32:48] = f[:, lanes]

    has = lambda flag: jnp.where(flag, 1, 0)
    partners = n_sub - 1
    for dr, dc in DIRS[2:]:
        partners = partners + has(exists(dr, dc))
    pl.semaphore_wait(barrier, partners)

    def remote(src_ref, dst_ref, send, recv, dr, dc=0):
        return pltpu.make_async_remote_copy(
            src_ref=src_ref, dst_ref=dst_ref, send_sem=send, recv_sem=recv,
            device_id={"sub": s + dr, "blk": b + dc}, device_id_type=MESH,
        )

    def a_copy(d):
        dr, dc = DIRS[d]
        if d < 2:
            pair_ = a_row_s.at[d], a_row_r.at[d]
        elif d < 4:
            pair_ = a_col_s.at[d - 2], a_col_r.at[d - 2]
        else:
            pair_ = a_cor_s.at[d - 4], a_cor_r.at[d - 4]
        return remote(*pair_, a_sem.at[0, d], a_sem.at[1, d], dr, dc)

    def b_copy(d):
        dr, dc = DIRS[d]
        pair_ = (b_row_s.at[d], b_row_r.at[d]) if d < 2 else (b_cor_s.at[d - 4], b_cor_r.at[d - 4])
        return remote(*pair_, b_sem.at[0, d], b_sem.at[1, d], dr, dc)

    row_bufs = ((x0_s, x0_r), (f1_s, f1_r), (x1_s, x1_r))

    def row_copy(e, d):
        send, recv = row_bufs[e]
        return remote(send.at[d], recv.at[d], row_sem.at[0, e, d], row_sem.at[1, e, d], DIRS[d][0])

    def row_start(e):
        for d in range(2):
            @pl.when(exists(*DIRS[d]))
            def _():
                row_copy(e, d).start()

    def row_wait(e, put):
        for d in range(2):
            @pl.when(exists(-DIRS[d][0], 0))
            def _():
                row_copy(e, d).wait_recv()
                put(d)

    def gather_copy(e, other, sender):
        buf = (cg2_g, f2_g)[e]
        return pltpu.make_async_remote_copy(
            src_ref=buf.at[sender], dst_ref=buf.at[sender],
            send_sem=gather_sem.at[0, e, other], recv_sem=gather_sem.at[1, e, sender],
            device_id={"sub": other}, device_id_type=MESH,
        )

    def gather_start(e):
        for other in range(n_sub):
            @pl.when(s != other)
            def _():
                gather_copy(e, other, s).start()

    def gather_wait(e):
        for other in range(n_sub):
            @pl.when(s != other)
            def _():
                gather_copy(e, other, other).wait_recv()

    for d in range(8):
        @pl.when(exists(*DIRS[d]))
        def _():
            a_copy(d).start()

    h1, own1 = halo // 2, own // 2
    both = jnp.concatenate([0.25 * c, g], axis=0)
    both = jnp.concatenate(coarsen(both, tmp), axis=1)
    c1[4:12, h1 : h1 + own1] = both[0:8]
    g1[4:12, h1 : h1 + own1] = both[8:16]
    for i, (rc, rg) in enumerate(((slice(0, 3), slice(8, 10)), (slice(5, 8), slice(14, 16)))):
        b_row_s[i, 0:3] = both[rc]
        b_row_s[i, 3:5] = both[rg]
        b_row_s[i, 5:8] = jnp.zeros((3, own1), jnp.float32)
        for j, lanes in enumerate((slice(0, h1), slice(own1 - h1, own1))):
            b_cor_s[2 * i + j, 0:3] = both[rc, lanes]
            b_cor_s[2 * i + j, 3:5] = both[rg, lanes]
            b_cor_s[2 * i + j, 5:8] = jnp.zeros((3, h1), jnp.float32)
    for d in (0, 1, 4, 5, 6, 7):
        @pl.when(exists(*DIRS[d]))
        def _():
            b_copy(d).start()

    for d, (dr, dc) in enumerate(DIRS):
        @pl.when(exists(-dr, -dc))
        def _():
            a_copy(d).wait_recv()
            lanes = {0: slice(halo, halo + own), 1: slice(0, halo), -1: slice(halo + own, w0)}[dc]
            if dr == 0:
                for k, ref in enumerate((c0, g0, f0)):
                    ref[4:20, lanes] = a_col_r[d - 2, 16 * k : 16 * k + 16]
            else:
                got = (a_row_r, d) if d < 2 else (a_cor_r, d - 4)
                got = got[0].at[got[1]]
                c0[slice(1, 4) if dr > 0 else slice(20, 23), lanes] = got[0:3]
                near = slice(2, 4) if dr > 0 else slice(20, 22)
                g0[near, lanes] = got[3:5]
                f0[near, lanes] = got[5:7]

    terms = chebyshev_terms(*SMOOTH)
    op0 = level_operator(c0[...], g0[...], False)
    f = f0[...]
    x = smooth(op0, f, None, terms)
    r = residual(op0, f, x)
    rhs = jnp.concatenate(coarsen(r[4:20], tmp), axis=1)
    f1[4:12, :] = rhs
    f1_s[0] = rhs[0:2]
    f1_s[1] = rhs[6:8]
    row_start(1)
    x0[...] = x
    x0_s[0] = x[4:6]
    x0_s[1] = x[18:20]
    row_start(0)

    sides = (slice(0, halo), slice(halo + own, w0))
    both = jnp.concatenate(
        [jnp.concatenate([0.25 * c0[4:20, v], g0[4:20, v]], axis=0) for v in sides], axis=1
    )
    both = jnp.concatenate(coarsen(both, tmp), axis=1)
    for k, lanes in enumerate((slice(0, h1), slice(h1 + own1, 2 * h1 + own1))):
        c1[4:12, lanes] = both[0:8, h1 * k : h1 * k + h1]
        g1[4:12, lanes] = both[8:16, h1 * k : h1 * k + h1]
    both = jnp.concatenate([0.25 * c1[4:12, :], g1[4:12, :]], axis=0)
    cg2_g[s] = jnp.concatenate(coarsen(both, tmp), axis=1)
    gather_start(0)
    for d in (0, 1, 4, 5, 6, 7):
        dr, dc = DIRS[d]
        @pl.when(exists(-dr, -dc))
        def _():
            b_copy(d).wait_recv()
            lanes = {0: slice(h1, h1 + own1), 1: slice(0, h1), -1: slice(h1 + own1, w1)}[dc]
            got = b_row_r.at[d] if d < 2 else b_cor_r.at[d - 4]
            c1[slice(1, 4) if dr > 0 else slice(12, 15), lanes] = got[0:3]
            g1[slice(2, 4) if dr > 0 else slice(12, 14), lanes] = got[3:5]
    op1 = level_operator(c1[...], g1[...], False)

    def put_f1(d):
        f1[slice(12, 14) if d == 0 else slice(2, 4), :] = f1_r[d]

    row_wait(1, put_f1)
    fl1 = f1[...]
    x = smooth(op1, fl1, None, terms)
    r = residual(op1, fl1, x)
    f2_g[s] = jnp.concatenate(coarsen(r[4:12], tmp), axis=1)
    gather_start(1)
    x1[...] = x
    x1_s[0] = x[4:7]
    x1_s[1] = x[9:12]
    row_start(2)

    gather_wait(0)
    for k in range(n_sub):
        c2[4 * k : 4 * k + 4, :] = cg2_g[k, 0:4]
        g2[4 * k : 4 * k + 4, :] = cg2_g[k, 4:8]

    cg = (c2[...], g2[...])
    ops = [level_operator(*cg, True)]
    rows = 4 * n_sub
    for level, width in ((3, w3), (4, w4)):
        rows //= 2
        full = max(rows, 8)
        parts = []
        for k, v in enumerate(cg):
            tiles = coarsen(0.25 * v if k == 0 else v, tmp)
            v = jnp.concatenate(tiles, axis=1)[:rows]
            if full > rows:
                v = jnp.concatenate([v, jnp.zeros((full - rows, width), jnp.float32)], axis=0)
            parts.append(v)
        cg = tuple(parts)
        ops.append(level_operator(*cg, True))

    gather_wait(1)
    for k in range(n_sub):
        f2[4 * k : 4 * k + 4, :] = f2_g[k]
    rhs = f2[...]
    kept = []
    rows = 4 * n_sub
    for level in (2, 3):
        op = ops[level - 2]
        x = smooth(op, rhs, None, terms)
        r = residual(op, rhs, x)
        kept.append((rhs, x))
        rows //= 2
        ref = (f3, f4)[level - 2]
        for j, tile in enumerate(coarsen(r, tmp)):
            ref[:rows, 128 * j : 128 * j + 128] = tile
        rhs = ref[...]
    y = smooth(ops[2], rhs, None, chebyshev_terms(coarse_count, COARSE_LOW, COARSE_HIGH))
    for level, width in ((3, w3), (2, w2)):
        op = ops[level - 2]
        rhs, x = kept[level - 2]
        rows = n_sub if level == 3 else 2 * n_sub
        y = x + op[6] * prolong(y, 0, rows, tmp_up, width)
        y = smooth(op, rhs, y, terms)

    for k in range(n_sub):
        y2[k + 1] = y[4 * k : 4 * k + 4]
    y = jnp.concatenate([y2[s][2:4], y2[s + 1], y2[s + 2][0:2]], axis=0)

    def put_x1(d):
        x1[slice(12, 15) if d == 0 else slice(1, 4), :] = x1_r[d]

    row_wait(2, put_x1)
    y = x1[...] + op1[6] * prolong(y, 0, 8, tmp_up, w1)
    y = smooth(op1, fl1, y, terms)

    def put_x0(d):
        x0[slice(20, 22) if d == 0 else slice(2, 4), :] = x0_r[d]

    row_wait(0, put_x0)
    y = x0[...] + op0[6] * prolong(y, 2, 12, tmp_up, w0)
    y = smooth(op0, f0[...], y, terms)
    out[...] = y[4:20, halo : halo + own]

    for d in range(8):
        @pl.when(exists(*DIRS[d]))
        def _():
            a_copy(d).wait_send()
    for d in (0, 1, 4, 5, 6, 7):
        @pl.when(exists(*DIRS[d]))
        def _():
            b_copy(d).wait_send()
    for e in range(3):
        for d in range(2):
            @pl.when(exists(*DIRS[d]))
            def _():
                row_copy(e, d).wait_send()
    for e in range(2):
        for other in range(n_sub):
            @pl.when(s != other)
            def _():
                gather_copy(e, other, s).wait_send()


def body(conductance, source_mask, ground_mask, nodata_mask):
    n_sub, n_blk = lax.axis_size("sub"), lax.axis_size("blk")
    rows, own = conductance.shape
    assert rows == 16 and own % 256 == 0
    coarse_count = 8 + n_sub // 2
    need = coarse_count + 2
    for _ in range(LEVELS - 1):
        need = 2 * need + 2
    halo = round_up(need, 256)
    assert halo <= own
    w0 = own + 2 * halo
    widths = (w0,) + tuple(round_up(w0 >> l, 128) for l in range(1, 5))
    w1, w2, w3, w4 = widths[1:]
    f32 = lambda *shape: pltpu.VMEM(shape, jnp.float32)
    i32 = lambda *shape: pltpu.VMEM(shape, jnp.int32)
    sem = lambda *shape: pltpu.SemaphoreType.DMA(shape)
    r2, r3, r4 = 4 * n_sub, max(2 * n_sub, 8), max(n_sub, 8)
    tmp_rows = max(32 * w0 // 128, 4 * n_sub * round_up(w2, 256) // 128)
    up_rows = max(24 * w0 // 128, 4 * n_sub * w2 // 128)
    vmem = pl.BlockSpec(memory_space=pltpu.VMEM)
    args = (conductance, source_mask, ground_mask, nodata_mask)
    args = [pltpu.with_memory_space_constraint(v, pltpu.HBM) for v in args]
    return pl.pallas_call(
        functools.partial(kernel, (n_sub, n_blk, halo, widths, coarse_count)),
        out_shape=jax.ShapeDtypeStruct((rows, own), jnp.float32),
        in_specs=[pl.BlockSpec(memory_space=pltpu.HBM)] * 4,
        out_specs=vmem,
        scratch_shapes=[
            f32(rows, own), i32(rows, own), i32(rows, own), i32(rows, own), sem(4),
            f32(24, w0), f32(24, w0), f32(24, w0), f32(24, w0),
            f32(16, w1), f32(16, w1), f32(16, w1), f32(16, w1),
            f32(r2, w2), f32(r2, w2), f32(r2, w2), f32(n_sub + 2, 4, w2),
            f32(r3, w3), f32(r4, w4), f32(tmp_rows, 128), f32(up_rows, 128),
            f32(2, 8, own), f32(2, 8, own), f32(2, 48, halo), f32(2, 48, halo),
            f32(4, 8, halo), f32(4, 8, halo), sem(2, 8),
            f32(2, 8, own // 2), f32(2, 8, own // 2), f32(4, 8, halo // 2), f32(4, 8, halo // 2), sem(2, 8),
            f32(2, 2, w0), f32(2, 2, w0),
            f32(2, 2, w1), f32(2, 2, w1), f32(2, 3, w1), f32(2, 3, w1), sem(2, 3, 2),
            f32(n_sub, 8, w2), f32(n_sub, 4, w2), sem(2, 2, n_sub),
        ],
        compiler_params=pltpu.CompilerParams(
            collective_id=0, has_side_effects=True, vmem_limit_bytes=40 * 1024 * 1024
        ),
    )(*args)


def solution(mesh):
    spec = P(("groups", "sub"), "blk")
    return jax.shard_map(
        body, mesh=mesh, in_specs=(spec,) * 4, out_specs=spec, check_vma=False
    )
```

```python
import functools
import jax
import jax.numpy as jnp
from jax import lax
from jax.experimental import pallas as pl
from jax.experimental.pallas import tpu as pltpu
from jax.sharding import PartitionSpec as P

LEVELS = 5
SMOOTH = (2, 0.5, 2.0)
COARSE_LOW, COARSE_HIGH = 0.02, 2.0
DIRS = ((-1, 0), (1, 0), (0, -1), (0, 1), (-1, -1), (-1, 1), (1, -1), (1, 1))
MESH = pl.DeviceIdType.MESH


def round_up(n, k):
    return -(-n // k) * k


def chebyshev_terms(sweep_count, low_end, high_end):
    mid = 0.5 * (high_end + low_end)
    half = 0.5 * (high_end - low_end)
    sigma = mid / half
    rho = 1.0 / sigma
    terms = [(0.0, 1.0 / mid)]
    for _ in range(1, sweep_count):
        rho_next = 1.0 / (2.0 * sigma - rho)
        terms.append((rho_next * rho, 2.0 * rho_next / half))
        rho = rho_next
    return terms


def rolled(x, shift, axis):
    return pltpu.roll(x, shift % x.shape[axis], axis)


def level_operator(c, g, whole_rows):
    rows, cols = c.shape
    h = 0.5 * c
    valid = c > 0.0
    c_r = rolled(c, -1, 1)
    c_d = rolled(c, -1, 0)
    e_r = jnp.where(valid & (c_r > 0.0), h + 0.5 * c_r, 0.0)
    ok_d = valid & (c_d > 0.0)
    if whole_rows:
        ok_d = ok_d & (lax.broadcasted_iota(jnp.int32, c.shape, 0) < rows - 1)
    e_d = jnp.where(ok_d, h + 0.5 * c_d, 0.0)
    e_l = rolled(e_r, 1, 1)
    e_u = rolled(e_d, 1, 0)
    m = jnp.where(valid, 1.0, 0.0)
    diag = e_d + e_u + e_r + e_l + g + (1.0 - m)
    inv = 1.0 / jnp.maximum(diag, 0.25 * c)
    return e_r, e_l, e_d, e_u, diag, inv, m


def residual(op, f, x):
    e_r, e_l, e_d, e_u, diag, inv, m = op
    across = e_r * rolled(x, -1, 1) + e_l * rolled(x, 1, 1)
    along = e_d * rolled(x, -1, 0) + e_u * rolled(x, 1, 0)
    return (f - diag * x) + (across + along)


def smooth(op, f, x, terms):
    d = None
    for keep, fresh in terms:
        r = f if x is None else residual(op, f, x)
        step = fresh * (r * op[5])
        d = step if d is None else keep * d + step
        x = d if x is None else x + d
    return x


def lane_take(x, which):
    lane = lax.broadcasted_iota(jnp.int32, x.shape, 1)
    if which == 0:
        index = jnp.bitwise_and(2 * lane, 127)
    else:
        index = jnp.right_shift(lane, 1) + 64 * (which - 1)
    return jnp.take_along_axis(x, index, axis=1, mode="promise_in_bounds")


def coarsen(x, tmp):
    rows, cols = x.shape
    k = round_up(cols, 256) // 256
    half = rows // 2
    sums = []
    for odd in range(2):
        base = odd * rows * k
        for j in range(k):
            lanes = 256 * j + 128 * odd
            if lanes < cols:
                tile = x[:, lanes : lanes + 128]
            else:
                tile = jnp.zeros((rows, 128), jnp.float32)
            tmp[base + rows * j : base + rows * (j + 1), :] = tile
        t = tmp[pl.ds(base, half * k, stride=2), :] + tmp[pl.ds(base + 1, half * k, stride=2), :]
        sums.append(lane_take(t + rolled(t, -1, 1), 0))
    lane = lax.broadcasted_iota(jnp.int32, sums[0].shape, 1)
    s = jnp.where(lane < 64, *sums)
    return [s[half * j : half * (j + 1)] for j in range(k)]


def prolong(x, first, rows, tmp, cols, skip=0):
    n = cols // 128 + skip
    for j in range(x.shape[1] // 128):
        tile = x[:, 128 * j : 128 * j + 128]
        for side in range(2):
            if skip <= 2 * j + side < n:
                base = 2 * rows * (2 * j + side)
                v = lane_take(tile, 1 + side)[first : first + rows]
                tmp[pl.ds(base, rows, stride=2), :] = v
                tmp[pl.ds(base + 1, rows, stride=2), :] = v
    return jnp.concatenate([tmp[2 * rows * j : 2 * rows * (j + 1), :] for j in range(skip, n)], axis=1)


def kernel(
    plan,
    cond_h, src_h, gnd_h, nod_h, out, cond, nod, gnd, src, in_sem,
    c0, g0, f0, x0, c1, g1, f1, x1, c2, g2, f2, y2, f3, f4, tmp, tmp_up,
    a_row_s, a_row_r, a_col_s, a_col_r, a_cor_s, a_cor_r, a_sem,
    b_row_s, b_row_r, b_cor_s, b_cor_r, b_sem,
    x0_s, x0_r, f1_s, f1_r, x1_s, x1_r, row_sem,
    cg2_g, f2_g, gather_sem,
):
    n_sub, n_blk, halo, widths, coarse_count = plan
    s, b = lax.axis_index("sub"), lax.axis_index("blk")
    w0, w1, w2, w3, w4 = widths
    own = out.shape[1]

    def exists(dr, dc):
        ok = None
        for need, cond_ in (
            (dr < 0, s > 0), (dr > 0, s < n_sub - 1), (dc < 0, b > 0), (dc > 0, b < n_blk - 1),
        ):
            if need:
                ok = cond_ if ok is None else ok & cond_
        return ok

    loads = [
        pltpu.make_async_copy(a, v, in_sem.at[i])
        for i, (a, v) in enumerate(((cond_h, cond), (nod_h, nod), (gnd_h, gnd), (src_h, src)))
    ]
    for load in loads:
        load.start()

    barrier = pltpu.get_barrier_semaphore()
    for dr in range(n_sub):
        @pl.when(s != dr)
        def _():
            pl.semaphore_signal(barrier, 1, device_id={"sub": dr}, device_id_type=MESH)
    for dr, dc in DIRS[2:]:
        @pl.when(exists(dr, dc))
        def _():
            pl.semaphore_signal(
                barrier, 1, device_id={"sub": s + dr, "blk": b + dc}, device_id_type=MESH
            )

    for ref in (c0, g0, f0, c1, g1, f1, y2, f3, f4):
        ref[...] = jnp.zeros_like(ref)

    for load in loads:
        load.wait()
    valid = 1.0 - nod[...].astype(jnp.float32)
    c = cond[...] * valid
    g = gnd[...].astype(jnp.float32) * c
    f = valid * (src[...].astype(jnp.float32) - 0.125)
    edges = ((slice(0, 3), slice(0, 2)), (slice(13, 16), slice(14, 16)))
    sides = (slice(0, halo), slice(own - halo, own))

    def stage(ref, rc, rg, lanes):
        ref[0:3] = c[rc, lanes]
        ref[3:5] = g[rg, lanes]
        ref[5:7] = f[rg, lanes]
        ref[7:8] = jnp.zeros((1, ref.shape[1]), jnp.float32)

    for i in range(2):
        stage(a_row_s.at[i], *edges[i], slice(0, own))

    has = lambda flag: jnp.where(flag, 1, 0)
    partners = n_sub - 1
    for dr, dc in DIRS[2:]:
        partners = partners + has(exists(dr, dc))
    pl.semaphore_wait(barrier, partners)

    def remote(src_ref, dst_ref, send, recv, dr, dc=0):
        return pltpu.make_async_remote_copy(
            src_ref=src_ref, dst_ref=dst_ref, send_sem=send, recv_sem=recv,
            device_id={"sub": s + dr, "blk": b + dc}, device_id_type=MESH,
        )

    def a_copy(d):
        dr, dc = DIRS[d]
        if d < 2:
            pair_ = a_row_s.at[d], a_row_r.at[d]
        elif d < 4:
            pair_ = a_col_s.at[d - 2], a_col_r.at[d - 2]
        else:
            pair_ = a_cor_s.at[d - 4], a_cor_r.at[d - 4]
        return remote(*pair_, a_sem.at[0, d], a_sem.at[1, d], dr, dc)

    def b_copy(d):
        dr, dc = DIRS[d]
        pair_ = (b_row_s.at[d], b_row_r.at[d]) if d < 2 else (b_cor_s.at[d - 4], b_cor_r.at[d - 4])
        return remote(*pair_, b_sem.at[0, d], b_sem.at[1, d], dr, dc)

    row_bufs = ((x0_s, x0_r), (f1_s, f1_r), (x1_s, x1_r))

    def row_copy(e, d):
        send, recv = row_bufs[e]
        return remote(send.at[d], recv.at[d], row_sem.at[0, e, d], row_sem.at[1, e, d], DIRS[d][0])

    def row_start(e):
        for d in range(2):
            @pl.when(exists(*DIRS[d]))
            def _():
                row_copy(e, d).start()

    def row_wait(e, put):
        for d in range(2):
            @pl.when(exists(-DIRS[d][0], 0))
            def _():
                row_copy(e, d).wait_recv()
                put(d)

    def gather_copy(e, other, sender):
        buf = (cg2_g, f2_g)[e]
        return pltpu.make_async_remote_copy(
            src_ref=buf.at[sender], dst_ref=buf.at[sender],
            send_sem=gather_sem.at[0, e, other], recv_sem=gather_sem.at[1, e, sender],
            device_id={"sub": other}, device_id_type=MESH,
        )

    def gather_start(e):
        for other in range(n_sub):
            @pl.when(s != other)
            def _():
                gather_copy(e, other, s).start()

    def row_done(e):
        for d in range(2):
            @pl.when(exists(*DIRS[d]))
            def _():
                row_copy(e, d).wait_send()

    def gather_done(e):
        for other in range(n_sub):
            @pl.when(s != other)
            def _():
                gather_copy(e, other, s).wait_send()

    def gather_wait(e):
        for other in range(n_sub):
            @pl.when(s != other)
            def _():
                gather_copy(e, other, other).wait_recv()

    def a_start(which):
        for d in which:
            @pl.when(exists(*DIRS[d]))
            def _():
                a_copy(d).start()

    a_start((0, 1))
    for j, lanes in enumerate(sides):
        for k, v in enumerate((c, g, f)):
            a_col_s[j, 16 * k : 16 * k + 16] = v[:, lanes]
    a_start((2, 3))
    for i in range(2):
        for j, lanes in enumerate(sides):
            stage(a_cor_s.at[2 * i + j], *edges[i], lanes)
    a_start((4, 5, 6, 7))
    c0[4:20, halo : halo + own] = c
    g0[4:20, halo : halo + own] = g
    f0[4:20, halo : halo + own] = f

    h1, own1 = halo // 2, own // 2
    both = jnp.concatenate([0.25 * c, g], axis=0)
    both = jnp.concatenate(coarsen(both, tmp), axis=1)
    c1[4:12, h1 : h1 + own1] = both[0:8]
    g1[4:12, h1 : h1 + own1] = both[8:16]
    for i, (rc, rg) in enumerate(((slice(0, 3), slice(8, 10)), (slice(5, 8), slice(14, 16)))):
        b_row_s[i, 0:3] = both[rc]
        b_row_s[i, 3:5] = both[rg]
        b_row_s[i, 5:8] = jnp.zeros((3, own1), jnp.float32)
        for j, lanes in enumerate((slice(0, h1), slice(own1 - h1, own1))):
            b_cor_s[2 * i + j, 0:3] = both[rc, lanes]
            b_cor_s[2 * i + j, 3:5] = both[rg, lanes]
            b_cor_s[2 * i + j, 5:8] = jnp.zeros((3, h1), jnp.float32)
    for d in (0, 1, 4, 5, 6, 7):
        @pl.when(exists(*DIRS[d]))
        def _():
            b_copy(d).start()

    for d, (dr, dc) in enumerate(DIRS):
        @pl.when(exists(-dr, -dc))
        def _():
            a_copy(d).wait_recv()
            lanes = {0: slice(halo, halo + own), 1: slice(0, halo), -1: slice(halo + own, w0)}[dc]
            if dr == 0:
                for k, ref in enumerate((c0, g0, f0)):
                    ref[4:20, lanes] = a_col_r[d - 2, 16 * k : 16 * k + 16]
            else:
                got = (a_row_r, d) if d < 2 else (a_cor_r, d - 4)
                got = got[0].at[got[1]]
                c0[slice(1, 4) if dr > 0 else slice(20, 23), lanes] = got[0:3]
                near = slice(2, 4) if dr > 0 else slice(20, 22)
                g0[near, lanes] = got[3:5]
                f0[near, lanes] = got[5:7]

    terms = chebyshev_terms(*SMOOTH)
    op0 = level_operator(c0[...], g0[...], False)
    f = f0[...]
    x = smooth(op0, f, None, terms)
    r = residual(op0, f, x)
    rhs = jnp.concatenate(coarsen(r[4:20], tmp), axis=1)
    f1[4:12, :] = rhs
    f1_s[0] = rhs[0:2]
    f1_s[1] = rhs[6:8]
    row_start(1)
    x0[...] = x
    x0_s[0] = x[4:6]
    x0_s[1] = x[18:20]
    row_start(0)

    sides = (slice(0, halo), slice(halo + own, w0))
    both = jnp.concatenate(
        [jnp.concatenate([0.25 * c0[4:20, v], g0[4:20, v]], axis=0) for v in sides], axis=1
    )
    both = jnp.concatenate(coarsen(both, tmp), axis=1)
    for k, lanes in enumerate((slice(0, h1), slice(h1 + own1, 2 * h1 + own1))):
        c1[4:12, lanes] = both[0:8, h1 * k : h1 * k + h1]
        g1[4:12, lanes] = both[8:16, h1 * k : h1 * k + h1]
    both = jnp.concatenate([0.25 * c1[4:12, :], g1[4:12, :]], axis=0)
    cg2_g[s] = jnp.concatenate(coarsen(both, tmp), axis=1)
    gather_start(0)
    for d in (0, 1, 4, 5, 6, 7):
        dr, dc = DIRS[d]
        @pl.when(exists(-dr, -dc))
        def _():
            b_copy(d).wait_recv()
            lanes = {0: slice(h1, h1 + own1), 1: slice(0, h1), -1: slice(h1 + own1, w1)}[dc]
            got = b_row_r.at[d] if d < 2 else b_cor_r.at[d - 4]
            c1[slice(1, 4) if dr > 0 else slice(12, 15), lanes] = got[0:3]
            g1[slice(2, 4) if dr > 0 else slice(12, 14), lanes] = got[3:5]
    op1 = level_operator(c1[...], g1[...], False)

    def put_f1(d):
        f1[slice(12, 14) if d == 0 else slice(2, 4), :] = f1_r[d]

    row_wait(1, put_f1)
    fl1 = f1[...]
    x = smooth(op1, fl1, None, terms)
    r = residual(op1, fl1, x)
    f2_g[s] = jnp.concatenate(coarsen(r[4:12], tmp), axis=1)
    gather_start(1)
    x1[...] = x
    x1_s[0] = x[4:7]
    x1_s[1] = x[9:12]
    row_start(2)

    for d in range(8):
        @pl.when(exists(*DIRS[d]))
        def _():
            a_copy(d).wait_send()
            if d not in (2, 3):
                b_copy(d).wait_send()
    row_done(0)
    row_done(1)
    gather_done(0)

    gather_wait(0)
    for k in range(n_sub):
        c2[4 * k : 4 * k + 4, :] = cg2_g[k, 0:4]
        g2[4 * k : 4 * k + 4, :] = cg2_g[k, 4:8]

    cg = (c2[...], g2[...])
    ops = [level_operator(*cg, True)]
    rows = 4 * n_sub
    for level, width in ((3, w3), (4, w4)):
        rows //= 2
        full = max(rows, 8)
        parts = []
        for k, v in enumerate(cg):
            tiles = coarsen(0.25 * v if k == 0 else v, tmp)
            v = jnp.concatenate(tiles, axis=1)[:rows]
            if full > rows:
                v = jnp.concatenate([v, jnp.zeros((full - rows, width), jnp.float32)], axis=0)
            parts.append(v)
        cg = tuple(parts)
        ops.append(level_operator(*cg, True))

    gather_wait(1)
    for k in range(n_sub):
        f2[4 * k : 4 * k + 4, :] = f2_g[k]
    rhs = f2[...]
    kept = []
    rows = 4 * n_sub
    for level in (2, 3):
        op = ops[level - 2]
        x = smooth(op, rhs, None, terms)
        r = residual(op, rhs, x)
        kept.append((rhs, x))
        rows //= 2
        ref = (f3, f4)[level - 2]
        for j, tile in enumerate(coarsen(r, tmp)):
            ref[:rows, 128 * j : 128 * j + 128] = tile
        rhs = ref[...]
    y = smooth(ops[2], rhs, None, chebyshev_terms(coarse_count, COARSE_LOW, COARSE_HIGH))
    for level, width in ((3, w3), (2, w2)):
        op = ops[level - 2]
        rhs, x = kept[level - 2]
        rows = n_sub if level == 3 else 2 * n_sub
        y = x + op[6] * prolong(y, 0, rows, tmp_up, width)
        y = smooth(op, rhs, y, terms)

    for k in range(n_sub):
        y2[k + 1] = y[4 * k : 4 * k + 4]
    y = jnp.concatenate([y2[s][2:4], y2[s + 1], y2[s + 2][0:2]], axis=0)

    def put_x1(d):
        x1[slice(12, 15) if d == 0 else slice(1, 4), :] = x1_r[d]

    row_wait(2, put_x1)
    y = x1[...] + op1[6] * prolong(y, 0, 8, tmp_up, w1)
    y = smooth(op1, fl1, y, terms)

    def put_x0(d):
        x0[slice(20, 22) if d == 0 else slice(2, 4), :] = x0_r[d]

    row_wait(0, put_x0)
    near = slice(halo - 128, halo + own + 128)
    op0 = [v[:, near] for v in op0]
    y = prolong(y, 2, 12, tmp_up, own + 256, halo // 128 - 1)
    y = smooth(op0, f0[:, near], x0[:, near] + op0[6] * y, terms)
    out[...] = y[4:20, 128 : 128 + own]

    row_done(2)
    gather_done(1)


def body(conductance, source_mask, ground_mask, nodata_mask):
    n_sub, n_blk = lax.axis_size("sub"), lax.axis_size("blk")
    rows, own = conductance.shape
    assert rows == 16 and own % 256 == 0
    coarse_count = 8 + n_sub // 2
    need = coarse_count + 2
    for _ in range(LEVELS - 1):
        need = 2 * need + 2
    halo = round_up(need, 256)
    assert halo <= own
    w0 = own + 2 * halo
    widths = (w0,) + tuple(round_up(w0 >> l, 128) for l in range(1, 5))
    w1, w2, w3, w4 = widths[1:]
    f32 = lambda *shape: pltpu.VMEM(shape, jnp.float32)
    i32 = lambda *shape: pltpu.VMEM(shape, jnp.int32)
    sem = lambda *shape: pltpu.SemaphoreType.DMA(shape)
    r2, r3, r4 = 4 * n_sub, max(2 * n_sub, 8), max(n_sub, 8)
    tmp_rows = max(32 * w0 // 128, 4 * n_sub * round_up(w2, 256) // 128)
    up_rows = max(24 * w0 // 128, 4 * n_sub * w2 // 128)
    vmem = pl.BlockSpec(memory_space=pltpu.VMEM)
    args = (conductance, source_mask, ground_mask, nodata_mask)
    args = [pltpu.with_memory_space_constraint(v, pltpu.HBM) for v in args]
    return pl.pallas_call(
        functools.partial(kernel, (n_sub, n_blk, halo, widths, coarse_count)),
        out_shape=jax.ShapeDtypeStruct((rows, own), jnp.float32),
        in_specs=[pl.BlockSpec(memory_space=pltpu.HBM)] * 4,
        out_specs=vmem,
        scratch_shapes=[
            f32(rows, own), i32(rows, own), i32(rows, own), i32(rows, own), sem(4),
            f32(24, w0), f32(24, w0), f32(24, w0), f32(24, w0),
            f32(16, w1), f32(16, w1), f32(16, w1), f32(16, w1),
            f32(r2, w2), f32(r2, w2), f32(r2, w2), f32(n_sub + 2, 4, w2),
            f32(r3, w3), f32(r4, w4), f32(tmp_rows, 128), f32(up_rows, 128),
            f32(2, 8, own), f32(2, 8, own), f32(2, 48, halo), f32(2, 48, halo),
            f32(4, 8, halo), f32(4, 8, halo), sem(2, 8),
            f32(2, 8, own // 2), f32(2, 8, own // 2), f32(4, 8, halo // 2), f32(4, 8, halo // 2), sem(2, 8),
            f32(2, 2, w0), f32(2, 2, w0),
            f32(2, 2, w1), f32(2, 2, w1), f32(2, 3, w1), f32(2, 3, w1), sem(2, 3, 2),
            f32(n_sub, 8, w2), f32(n_sub, 4, w2), sem(2, 2, n_sub),
        ],
        compiler_params=pltpu.CompilerParams(
            collective_id=0, has_side_effects=True, vmem_limit_bytes=40 * 1024 * 1024
        ),
    )(*args)


def solution(mesh):
    spec = P(("groups", "sub"), "blk")
    return jax.shard_map(
        body, mesh=mesh, in_specs=(spec,) * 4, out_specs=spec, check_vma=False
    )
```

```python
import functools
import jax
import jax.numpy as jnp
from jax import lax
from jax.experimental import pallas as pl
from jax.experimental.pallas import tpu as pltpu
from jax.sharding import PartitionSpec as P

LEVELS = 5
SMOOTH = (2, 0.5, 2.0)
COARSE_LOW, COARSE_HIGH = 0.02, 2.0
DIRS = ((-1, 0), (1, 0), (0, -1), (0, 1), (-1, -1), (-1, 1), (1, -1), (1, 1))
MESH = pl.DeviceIdType.MESH


def round_up(n, k):
    return -(-n // k) * k


def chebyshev_terms(sweep_count, low_end, high_end):
    mid = 0.5 * (high_end + low_end)
    half = 0.5 * (high_end - low_end)
    sigma = mid / half
    rho = 1.0 / sigma
    terms = [(0.0, 1.0 / mid)]
    for _ in range(1, sweep_count):
        rho_next = 1.0 / (2.0 * sigma - rho)
        terms.append((rho_next * rho, 2.0 * rho_next / half))
        rho = rho_next
    return terms


def rolled(x, shift, axis):
    return pltpu.roll(x, shift % x.shape[axis], axis)


def level_operator(c, g, whole_rows):
    rows, cols = c.shape
    h = 0.5 * c
    valid = c > 0.0
    c_r = rolled(c, -1, 1)
    c_d = rolled(c, -1, 0)
    e_r = jnp.where(valid & (c_r > 0.0), h + 0.5 * c_r, 0.0)
    ok_d = valid & (c_d > 0.0)
    if whole_rows:
        ok_d = ok_d & (lax.broadcasted_iota(jnp.int32, c.shape, 0) < rows - 1)
    e_d = jnp.where(ok_d, h + 0.5 * c_d, 0.0)
    e_l = rolled(e_r, 1, 1)
    e_u = rolled(e_d, 1, 0)
    m = jnp.where(valid, 1.0, 0.0)
    diag = e_d + e_u + e_r + e_l + g + (1.0 - m)
    inv = 1.0 / jnp.maximum(diag, 0.25 * c)
    return e_r, e_l, e_d, e_u, diag, inv, m


def residual(op, f, x):
    e_r, e_l, e_d, e_u, diag, inv, m = op
    across = e_r * rolled(x, -1, 1) + e_l * rolled(x, 1, 1)
    along = e_d * rolled(x, -1, 0) + e_u * rolled(x, 1, 0)
    return (f - diag * x) + (across + along)


def smooth(op, f, x, terms):
    d = None
    for keep, fresh in terms:
        r = f if x is None else residual(op, f, x)
        step = fresh * (r * op[5])
        d = step if d is None else keep * d + step
        x = d if x is None else x + d
    return x


def lane_take(x, which):
    lane = lax.broadcasted_iota(jnp.int32, x.shape, 1)
    if which == 0:
        index = jnp.bitwise_and(2 * lane, 127)
    else:
        index = jnp.right_shift(lane, 1) + 64 * (which - 1)
    return jnp.take_along_axis(x, index, axis=1, mode="promise_in_bounds")


def coarsen(x, tmp):
    rows, cols = x.shape
    k = round_up(cols, 256) // 256
    half = rows // 2
    sums = []
    for odd in range(2):
        base = odd * rows * k
        for j in range(k):
            lanes = 256 * j + 128 * odd
            if lanes < cols:
                tile = x[:, lanes : lanes + 128]
            else:
                tile = jnp.zeros((rows, 128), jnp.float32)
            tmp[base + rows * j : base + rows * (j + 1), :] = tile
        t = tmp[pl.ds(base, half * k, stride=2), :] + tmp[pl.ds(base + 1, half * k, stride=2), :]
        sums.append(lane_take(t + rolled(t, -1, 1), 0))
    lane = lax.broadcasted_iota(jnp.int32, sums[0].shape, 1)
    s = jnp.where(lane < 64, *sums)
    return [s[half * j : half * (j + 1)] for j in range(k)]


def prolong(x, first, rows, tmp, cols, skip=0):
    n = cols // 128 + skip
    for j in range(x.shape[1] // 128):
        tile = x[:, 128 * j : 128 * j + 128]
        for side in range(2):
            if skip <= 2 * j + side < n:
                base = 2 * rows * (2 * j + side)
                v = lane_take(tile, 1 + side)[first : first + rows]
                tmp[pl.ds(base, rows, stride=2), :] = v
                tmp[pl.ds(base + 1, rows, stride=2), :] = v
    return jnp.concatenate([tmp[2 * rows * j : 2 * rows * (j + 1), :] for j in range(skip, n)], axis=1)


def kernel(
    plan,
    cond_h, src_h, gnd_h, nod_h, out, cond, nod, gnd, src, in_sem,
    c0_all, g0_all, f0_all, x0_all, op0, c1, g1, f1, x1, c2, g2, f2, y2, f3, f4, tmp, tmp_up,
    a_row_s, a_row_r, a_col_s, a_col_r, a_cor_s, a_cor_r, a_sem,
    b_row_s, b_row_r, b_cor_s, b_cor_r, b_sem,
    x0_s, x0_r, f1_s, f1_r, x1_s, x1_r, row_sem,
    cg2_g, f2_g, gather_sem,
):
    n_sub, n_blk, halo, widths, coarse_count = plan
    s, b = lax.axis_index("sub"), lax.axis_index("blk")
    w0, w1, w2, w3, w4 = widths
    own = out.shape[1]
    c0, g0, f0, x0 = (v.at[:, pl.ds(128, w0)] for v in (c0_all, g0_all, f0_all, x0_all))

    def exists(dr, dc):
        ok = None
        for need, cond_ in (
            (dr < 0, s > 0), (dr > 0, s < n_sub - 1), (dc < 0, b > 0), (dc > 0, b < n_blk - 1),
        ):
            if need:
                ok = cond_ if ok is None else ok & cond_
        return ok

    loads = [
        pltpu.make_async_copy(a, v, in_sem.at[i])
        for i, (a, v) in enumerate(((cond_h, cond), (nod_h, nod), (gnd_h, gnd), (src_h, src)))
    ]
    for load in loads:
        load.start()

    barrier = pltpu.get_barrier_semaphore()
    for dr in range(n_sub):
        @pl.when(s != dr)
        def _():
            pl.semaphore_signal(barrier, 1, device_id={"sub": dr}, device_id_type=MESH)
    for dr, dc in DIRS[2:]:
        @pl.when(exists(dr, dc))
        def _():
            pl.semaphore_signal(
                barrier, 1, device_id={"sub": s + dr, "blk": b + dc}, device_id_type=MESH
            )

    for ref in (c0_all, g0_all, f0_all, c1, g1, f1, y2, f3, f4):
        ref[...] = jnp.zeros_like(ref)

    for load in loads:
        load.wait()
    valid = 1.0 - nod[...].astype(jnp.float32)
    c = cond[...] * valid
    g = gnd[...].astype(jnp.float32) * c
    f = valid * (src[...].astype(jnp.float32) - 0.125)
    edges = ((slice(0, 3), slice(0, 2)), (slice(13, 16), slice(14, 16)))
    sides = (slice(0, halo), slice(own - halo, own))

    def stage(ref, rc, rg, lanes):
        ref[0:3] = c[rc, lanes]
        ref[3:5] = g[rg, lanes]
        ref[5:7] = f[rg, lanes]
        ref[7:8] = jnp.zeros((1, ref.shape[1]), jnp.float32)

    for i in range(2):
        stage(a_row_s.at[i], *edges[i], slice(0, own))

    has = lambda flag: jnp.where(flag, 1, 0)
    partners = n_sub - 1
    for dr, dc in DIRS[2:]:
        partners = partners + has(exists(dr, dc))
    pl.semaphore_wait(barrier, partners)

    def remote(src_ref, dst_ref, send, recv, dr, dc=0):
        return pltpu.make_async_remote_copy(
            src_ref=src_ref, dst_ref=dst_ref, send_sem=send, recv_sem=recv,
            device_id={"sub": s + dr, "blk": b + dc}, device_id_type=MESH,
        )

    def a_copy(d):
        dr, dc = DIRS[d]
        if d < 2:
            pair_ = a_row_s.at[d], a_row_r.at[d]
        elif d < 4:
            pair_ = a_col_s.at[d - 2], a_col_r.at[d - 2]
        else:
            pair_ = a_cor_s.at[d - 4], a_cor_r.at[d - 4]
        return remote(*pair_, a_sem.at[0, d], a_sem.at[1, d], dr, dc)

    def b_copy(d):
        dr, dc = DIRS[d]
        pair_ = (b_row_s.at[d], b_row_r.at[d]) if d < 2 else (b_cor_s.at[d - 4], b_cor_r.at[d - 4])
        return remote(*pair_, b_sem.at[0, d], b_sem.at[1, d], dr, dc)

    row_bufs = ((x0_s, x0_r), (f1_s, f1_r), (x1_s, x1_r))

    def row_copy(e, d):
        send, recv = row_bufs[e]
        return remote(send.at[d], recv.at[d], row_sem.at[0, e, d], row_sem.at[1, e, d], DIRS[d][0])

    def row_start(e):
        for d in range(2):
            @pl.when(exists(*DIRS[d]))
            def _():
                row_copy(e, d).start()

    def row_wait(e, put):
        for d in range(2):
            @pl.when(exists(-DIRS[d][0], 0))
            def _():
                row_copy(e, d).wait_recv()
                put(d)

    def gather_copy(e, other, sender):
        buf = (cg2_g, f2_g)[e]
        return pltpu.make_async_remote_copy(
            src_ref=buf.at[sender], dst_ref=buf.at[sender],
            send_sem=gather_sem.at[0, e, other], recv_sem=gather_sem.at[1, e, sender],
            device_id={"sub": other}, device_id_type=MESH,
        )

    def gather_start(e):
        for other in range(n_sub):
            @pl.when(s != other)
            def _():
                gather_copy(e, other, s).start()

    def row_done(e):
        for d in range(2):
            @pl.when(exists(*DIRS[d]))
            def _():
                row_copy(e, d).wait_send()

    def gather_done(e):
        for other in range(n_sub):
            @pl.when(s != other)
            def _():
                gather_copy(e, other, s).wait_send()

    def gather_wait(e):
        for other in range(n_sub):
            @pl.when(s != other)
            def _():
                gather_copy(e, other, other).wait_recv()

    def a_start(which):
        for d in which:
            @pl.when(exists(*DIRS[d]))
            def _():
                a_copy(d).start()

    a_start((0, 1))
    for j, lanes in enumerate(sides):
        for k, v in enumerate((c, g, f)):
            a_col_s[j, 16 * k : 16 * k + 16] = v[:, lanes]
    a_start((2, 3))
    for i in range(2):
        for j, lanes in enumerate(sides):
            stage(a_cor_s.at[2 * i + j], *edges[i], lanes)
    a_start((4, 5, 6, 7))
    c0[4:20, halo : halo + own] = c
    g0[4:20, halo : halo + own] = g
    f0[4:20, halo : halo + own] = f

    h1, own1 = halo // 2, own // 2
    both = jnp.concatenate([0.25 * c, g], axis=0)
    both = jnp.concatenate(coarsen(both, tmp), axis=1)
    c1[4:12, h1 : h1 + own1] = both[0:8]
    g1[4:12, h1 : h1 + own1] = both[8:16]
    for i, (rc, rg) in enumerate(((slice(0, 3), slice(8, 10)), (slice(5, 8), slice(14, 16)))):
        b_row_s[i, 0:3] = both[rc]
        b_row_s[i, 3:5] = both[rg]
        b_row_s[i, 5:8] = jnp.zeros((3, own1), jnp.float32)
        for j, lanes in enumerate((slice(0, h1), slice(own1 - h1, own1))):
            b_cor_s[2 * i + j, 0:3] = both[rc, lanes]
            b_cor_s[2 * i + j, 3:5] = both[rg, lanes]
            b_cor_s[2 * i + j, 5:8] = jnp.zeros((3, h1), jnp.float32)
    for d in (0, 1, 4, 5, 6, 7):
        @pl.when(exists(*DIRS[d]))
        def _():
            b_copy(d).start()

    for d, (dr, dc) in enumerate(DIRS):
        @pl.when(exists(-dr, -dc))
        def _():
            a_copy(d).wait_recv()
            lanes = {0: slice(halo, halo + own), 1: slice(0, halo), -1: slice(halo + own, w0)}[dc]
            if dr == 0:
                for k, ref in enumerate((c0, g0, f0)):
                    ref[4:20, lanes] = a_col_r[d - 2, 16 * k : 16 * k + 16]
            else:
                got = (a_row_r, d) if d < 2 else (a_cor_r, d - 4)
                got = got[0].at[got[1]]
                c0[slice(1, 4) if dr > 0 else slice(20, 23), lanes] = got[0:3]
                near = slice(2, 4) if dr > 0 else slice(20, 22)
                g0[near, lanes] = got[3:5]
                f0[near, lanes] = got[5:7]

    terms = chebyshev_terms(*SMOOTH)
    @pl.loop(0, w0 // 512)
    def _(i):
        window = pl.ds(pl.multiple_of(i * 512, 128), 768)
        inner = pl.ds(pl.multiple_of(i * 512 + 128, 128), 512)
        op = level_operator(c0_all[:, window], g0_all[:, window], False)
        f = f0_all[:, window]
        x = smooth(op, f, None, terms)
        r = residual(op, f, x)
        tiles = coarsen(r[4:20, 128:640], tmp)
        f1[4:12, pl.ds(pl.multiple_of(i * 256, 128), 256)] = jnp.concatenate(tiles, axis=1)
        x0_all[:, inner] = x[:, 128:640]
        for k, v in enumerate(op):
            op0[k, :, inner] = v[:, 128:640]

    f1_s[0] = f1[4:6, :]
    f1_s[1] = f1[10:12, :]
    row_start(1)
    x0_s[0] = x0[4:6, :]
    x0_s[1] = x0[18:20, :]
    row_start(0)

    sides = (slice(0, halo), slice(halo + own, w0))
    both = jnp.concatenate(
        [jnp.concatenate([0.25 * c0[4:20, v], g0[4:20, v]], axis=0) for v in sides], axis=1
    )
    both = jnp.concatenate(coarsen(both, tmp), axis=1)
    for k, lanes in enumerate((slice(0, h1), slice(h1 + own1, 2 * h1 + own1))):
        c1[4:12, lanes] = both[0:8, h1 * k : h1 * k + h1]
        g1[4:12, lanes] = both[8:16, h1 * k : h1 * k + h1]
    both = jnp.concatenate([0.25 * c1[4:12, :], g1[4:12, :]], axis=0)
    cg2_g[s] = jnp.concatenate(coarsen(both, tmp), axis=1)
    gather_start(0)
    for d in (0, 1, 4, 5, 6, 7):
        dr, dc = DIRS[d]
        @pl.when(exists(-dr, -dc))
        def _():
            b_copy(d).wait_recv()
            lanes = {0: slice(h1, h1 + own1), 1: slice(0, h1), -1: slice(h1 + own1, w1)}[dc]
            got = b_row_r.at[d] if d < 2 else b_cor_r.at[d - 4]
            c1[slice(1, 4) if dr > 0 else slice(12, 15), lanes] = got[0:3]
            g1[slice(2, 4) if dr > 0 else slice(12, 14), lanes] = got[3:5]
    op1 = level_operator(c1[...], g1[...], False)

    def put_f1(d):
        f1[slice(12, 14) if d == 0 else slice(2, 4), :] = f1_r[d]

    row_wait(1, put_f1)
    fl1 = f1[...]
    x = smooth(op1, fl1, None, terms)
    r = residual(op1, fl1, x)
    f2_g[s] = jnp.concatenate(coarsen(r[4:12], tmp), axis=1)
    gather_start(1)
    x1[...] = x
    x1_s[0] = x[4:7]
    x1_s[1] = x[9:12]
    row_start(2)

    for d in range(8):
        @pl.when(exists(*DIRS[d]))
        def _():
            a_copy(d).wait_send()
            if d not in (2, 3):
                b_copy(d).wait_send()
    row_done(0)
    row_done(1)
    gather_done(0)

    gather_wait(0)
    for k in range(n_sub):
        c2[4 * k : 4 * k + 4, :] = cg2_g[k, 0:4]
        g2[4 * k : 4 * k + 4, :] = cg2_g[k, 4:8]

    cg = (c2[...], g2[...])
    ops = [level_operator(*cg, True)]
    rows = 4 * n_sub
    for level, width in ((3, w3), (4, w4)):
        rows //= 2
        full = max(rows, 8)
        parts = []
        for k, v in enumerate(cg):
            tiles = coarsen(0.25 * v if k == 0 else v, tmp)
            v = jnp.concatenate(tiles, axis=1)[:rows]
            if full > rows:
                v = jnp.concatenate([v, jnp.zeros((full - rows, width), jnp.float32)], axis=0)
            parts.append(v)
        cg = tuple(parts)
        ops.append(level_operator(*cg, True))

    gather_wait(1)
    for k in range(n_sub):
        f2[4 * k : 4 * k + 4, :] = f2_g[k]
    rhs = f2[...]
    kept = []
    rows = 4 * n_sub
    for level in (2, 3):
        op = ops[level - 2]
        x = smooth(op, rhs, None, terms)
        r = residual(op, rhs, x)
        kept.append((rhs, x))
        rows //= 2
        ref = (f3, f4)[level - 2]
        for j, tile in enumerate(coarsen(r, tmp)):
            ref[:rows, 128 * j : 128 * j + 128] = tile
        rhs = ref[...]
    y = smooth(ops[2], rhs, None, chebyshev_terms(coarse_count, COARSE_LOW, COARSE_HIGH))
    for level, width in ((3, w3), (2, w2)):
        op = ops[level - 2]
        rhs, x = kept[level - 2]
        rows = n_sub if level == 3 else 2 * n_sub
        y = x + op[6] * prolong(y, 0, rows, tmp_up, width)
        y = smooth(op, rhs, y, terms)

    for k in range(n_sub):
        y2[k + 1] = y[4 * k : 4 * k + 4]
    y = jnp.concatenate([y2[s][2:4], y2[s + 1], y2[s + 2][0:2]], axis=0)

    def put_x1(d):
        x1[slice(12, 15) if d == 0 else slice(1, 4), :] = x1_r[d]

    row_wait(2, put_x1)
    y = x1[...] + op1[6] * prolong(y, 0, 8, tmp_up, w1)
    y = smooth(op1, fl1, y, terms)

    def put_x0(d):
        x0[slice(20, 22) if d == 0 else slice(2, 4), :] = x0_r[d]

    row_wait(0, put_x0)
    x1[...] = y

    @pl.loop(0, own // 512)
    def _(i):
        window = pl.ds(pl.multiple_of(halo + i * 512, 128), 768)
        lanes = pl.ds(pl.multiple_of(halo // 2 - 128 + i * 256, 128), 512)
        op = [op0[k, :, window] for k in range(7)]
        y = x0_all[:, window] + op[6] * prolong(x1[:, lanes], 2, 12, tmp_up, 768, 1)
        y = smooth(op, f0_all[:, window], y, terms)
        out[:, pl.ds(pl.multiple_of(i * 512, 128), 512)] = y[4:20, 128:640]

    row_done(2)
    gather_done(1)


def body(conductance, source_mask, ground_mask, nodata_mask):
    n_sub, n_blk = lax.axis_size("sub"), lax.axis_size("blk")
    rows, own = conductance.shape
    assert rows == 16 and own % 512 == 0
    coarse_count = 8 + n_sub // 2
    need = coarse_count + 2
    for _ in range(LEVELS - 1):
        need = 2 * need + 2
    halo = round_up(need, 256)
    assert halo <= own
    w0 = own + 2 * halo
    widths = (w0,) + tuple(round_up(w0 >> l, 128) for l in range(1, 5))
    w1, w2, w3, w4 = widths[1:]
    f32 = lambda *shape: pltpu.VMEM(shape, jnp.float32)
    i32 = lambda *shape: pltpu.VMEM(shape, jnp.int32)
    sem = lambda *shape: pltpu.SemaphoreType.DMA(shape)
    r2, r3, r4 = 4 * n_sub, max(2 * n_sub, 8), max(n_sub, 8)
    tmp_rows = max(32 * w0 // 128, 4 * n_sub * round_up(w2, 256) // 128)
    up_rows = max(24 * w0 // 128, 4 * n_sub * w2 // 128)
    vmem = pl.BlockSpec(memory_space=pltpu.VMEM)
    args = (conductance, source_mask, ground_mask, nodata_mask)
    args = [pltpu.with_memory_space_constraint(v, pltpu.HBM) for v in args]
    return pl.pallas_call(
        functools.partial(kernel, (n_sub, n_blk, halo, widths, coarse_count)),
        out_shape=jax.ShapeDtypeStruct((rows, own), jnp.float32),
        in_specs=[pl.BlockSpec(memory_space=pltpu.HBM)] * 4,
        out_specs=vmem,
        scratch_shapes=[
            f32(rows, own), i32(rows, own), i32(rows, own), i32(rows, own), sem(4),
            f32(24, w0 + 256), f32(24, w0 + 256), f32(24, w0 + 256), f32(24, w0 + 256),
            f32(7, 24, w0 + 256),
            f32(16, w1), f32(16, w1), f32(16, w1), f32(16, w1),
            f32(r2, w2), f32(r2, w2), f32(r2, w2), f32(n_sub + 2, 4, w2),
            f32(r3, w3), f32(r4, w4), f32(tmp_rows, 128), f32(up_rows, 128),
            f32(2, 8, own), f32(2, 8, own), f32(2, 48, halo), f32(2, 48, halo),
            f32(4, 8, halo), f32(4, 8, halo), sem(2, 8),
            f32(2, 8, own // 2), f32(2, 8, own // 2), f32(4, 8, halo // 2), f32(4, 8, halo // 2), sem(2, 8),
            f32(2, 2, w0), f32(2, 2, w0),
            f32(2, 2, w1), f32(2, 2, w1), f32(2, 3, w1), f32(2, 3, w1), sem(2, 3, 2),
            f32(n_sub, 8, w2), f32(n_sub, 4, w2), sem(2, 2, n_sub),
        ],
        compiler_params=pltpu.CompilerParams(
            collective_id=0, has_side_effects=True, vmem_limit_bytes=40 * 1024 * 1024
        ),
    )(*args)


def solution(mesh):
    spec = P(("groups", "sub"), "blk")
    return jax.shard_map(
        body, mesh=mesh, in_specs=(spec,) * 4, out_specs=spec, check_vma=False
    )
```

```python
import functools
import jax
import jax.numpy as jnp
from jax import lax
from jax.experimental import pallas as pl
from jax.experimental.pallas import tpu as pltpu
from jax.sharding import PartitionSpec as P

LEVELS = 5
SMOOTH = (2, 0.5, 2.0)
COARSE_LOW, COARSE_HIGH = 0.02, 2.0
DIRS = ((-1, 0), (1, 0), (0, -1), (0, 1), (-1, -1), (-1, 1), (1, -1), (1, 1))
MESH = pl.DeviceIdType.MESH


def round_up(n, k):
    return -(-n // k) * k


def chebyshev_terms(sweep_count, low_end, high_end):
    mid = 0.5 * (high_end + low_end)
    half = 0.5 * (high_end - low_end)
    sigma = mid / half
    rho = 1.0 / sigma
    terms = [(0.0, 1.0 / mid)]
    for _ in range(1, sweep_count):
        rho_next = 1.0 / (2.0 * sigma - rho)
        terms.append((rho_next * rho, 2.0 * rho_next / half))
        rho = rho_next
    return terms


def rolled(x, shift, axis):
    return pltpu.roll(x, shift % x.shape[axis], axis)


def row_neighbours(x, spare):
    if spare is None:
        return rolled(x, 1, 0), rolled(x, -1, 0)
    rows, tiles = x.shape[0], x.shape[1] // 128
    for t in range(tiles):
        spare[t, 8 : 8 + rows, :] = x[:, 128 * t : 128 * t + 128]
    return [
        jnp.concatenate([spare[t, at : at + rows, :] for t in range(tiles)], axis=1)
        for at in (7, 9)
    ]


def level_operator(c, g, whole_rows, spare=None):
    rows, cols = c.shape
    h = 0.5 * c
    valid = c > 0.0
    c_r = rolled(c, -1, 1)
    c_d = row_neighbours(c, spare)[1]
    e_r = jnp.where(valid & (c_r > 0.0), h + 0.5 * c_r, 0.0)
    ok_d = valid & (c_d > 0.0)
    if whole_rows:
        ok_d = ok_d & (lax.broadcasted_iota(jnp.int32, c.shape, 0) < rows - 1)
    e_d = jnp.where(ok_d, h + 0.5 * c_d, 0.0)
    e_l = rolled(e_r, 1, 1)
    e_u = row_neighbours(e_d, spare)[0]
    m = jnp.where(valid, 1.0, 0.0)
    diag = e_d + e_u + e_r + e_l + g + (1.0 - m)
    inv = 1.0 / jnp.maximum(diag, 0.25 * c)
    return e_r, e_l, e_d, e_u, diag, inv, m


def residual(op, f, x, spare=None):
    e_r, e_l, e_d, e_u, diag, inv, m = op
    across = e_r * rolled(x, -1, 1) + e_l * rolled(x, 1, 1)
    x_u, x_d = row_neighbours(x, spare)
    along = e_d * x_d + e_u * x_u
    return (f - diag * x) + (across + along)


def smooth(op, f, x, terms, spare=None):
    d = None
    for keep, fresh in terms:
        r = f if x is None else residual(op, f, x, spare)
        step = fresh * (r * op[5])
        d = step if d is None else keep * d + step
        x = d if x is None else x + d
    return x


def lane_take(x, which):
    lane = lax.broadcasted_iota(jnp.int32, x.shape, 1)
    if which == 0:
        index = jnp.bitwise_and(2 * lane, 127)
    else:
        index = jnp.right_shift(lane, 1) + 64 * (which - 1)
    return jnp.take_along_axis(x, index, axis=1, mode="promise_in_bounds")


def coarsen(x, tmp):
    rows, cols = x.shape
    k = round_up(cols, 256) // 256
    half = rows // 2
    sums = []
    for odd in range(2):
        base = odd * rows * k
        for j in range(k):
            lanes = 256 * j + 128 * odd
            if lanes < cols:
                tile = x[:, lanes : lanes + 128]
            else:
                tile = jnp.zeros((rows, 128), jnp.float32)
            tmp[base + rows * j : base + rows * (j + 1), :] = tile
        t = tmp[pl.ds(base, half * k, stride=2), :] + tmp[pl.ds(base + 1, half * k, stride=2), :]
        sums.append(lane_take(t + rolled(t, -1, 1), 0))
    lane = lax.broadcasted_iota(jnp.int32, sums[0].shape, 1)
    s = jnp.where(lane < 64, *sums)
    return [s[half * j : half * (j + 1)] for j in range(k)]


def prolong(x, first, rows, tmp, cols, skip=0):
    n = cols // 128 + skip
    for j in range(x.shape[1] // 128):
        tile = x[:, 128 * j : 128 * j + 128]
        for side in range(2):
            if skip <= 2 * j + side < n:
                base = 2 * rows * (2 * j + side)
                v = lane_take(tile, 1 + side)[first : first + rows]
                tmp[pl.ds(base, rows, stride=2), :] = v
                tmp[pl.ds(base + 1, rows, stride=2), :] = v
    return jnp.concatenate([tmp[2 * rows * j : 2 * rows * (j + 1), :] for j in range(skip, n)], axis=1)


def kernel(
    plan,
    cond_h, src_h, gnd_h, nod_h, out, cond, nod, gnd, src, in_sem,
    spare0, spare1, c0, g0, f0, x0, c1, g1, f1, x1, c2, g2, f2, y2, f3, f4, tmp, tmp_up,
    a_row_s, a_row_r, a_col_s, a_col_r, a_cor_s, a_cor_r, a_sem,
    b_row_s, b_row_r, b_cor_s, b_cor_r, b_sem,
    x0_s, x0_r, f1_s, f1_r, x1_s, x1_r, row_sem,
    cg2_g, f2_g, gather_sem,
):
    n_sub, n_blk, halo, widths, coarse_count = plan
    s, b = lax.axis_index("sub"), lax.axis_index("blk")
    w0, w1, w2, w3, w4 = widths
    own = out.shape[1]

    def exists(dr, dc):
        ok = None
        for need, cond_ in (
            (dr < 0, s > 0), (dr > 0, s < n_sub - 1), (dc < 0, b > 0), (dc > 0, b < n_blk - 1),
        ):
            if need:
                ok = cond_ if ok is None else ok & cond_
        return ok

    loads = [
        pltpu.make_async_copy(a, v, in_sem.at[i])
        for i, (a, v) in enumerate(((cond_h, cond), (nod_h, nod), (gnd_h, gnd), (src_h, src)))
    ]
    for load in loads:
        load.start()

    barrier = pltpu.get_barrier_semaphore()
    for dr in range(n_sub):
        @pl.when(s != dr)
        def _():
            pl.semaphore_signal(barrier, 1, device_id={"sub": dr}, device_id_type=MESH)
    for dr, dc in DIRS[2:]:
        @pl.when(exists(dr, dc))
        def _():
            pl.semaphore_signal(
                barrier, 1, device_id={"sub": s + dr, "blk": b + dc}, device_id_type=MESH
            )

    for ref in (spare0, spare1, c0, g0, f0, c1, g1, f1, y2, f3, f4):
        ref[...] = jnp.zeros_like(ref)

    for load in loads:
        load.wait()
    valid = 1.0 - nod[...].astype(jnp.float32)
    c = cond[...] * valid
    g = gnd[...].astype(jnp.float32) * c
    f = valid * (src[...].astype(jnp.float32) - 0.125)
    edges = ((slice(0, 3), slice(0, 2)), (slice(13, 16), slice(14, 16)))
    sides = (slice(0, halo), slice(own - halo, own))

    def stage(ref, rc, rg, lanes):
        ref[0:3] = c[rc, lanes]
        ref[3:5] = g[rg, lanes]
        ref[5:7] = f[rg, lanes]
        ref[7:8] = jnp.zeros((1, ref.shape[1]), jnp.float32)

    for i in range(2):
        stage(a_row_s.at[i], *edges[i], slice(0, own))

    has = lambda flag: jnp.where(flag, 1, 0)
    partners = n_sub - 1
    for dr, dc in DIRS[2:]:
        partners = partners + has(exists(dr, dc))
    pl.semaphore_wait(barrier, partners)

    def remote(src_ref, dst_ref, send, recv, dr, dc=0):
        return pltpu.make_async_remote_copy(
            src_ref=src_ref, dst_ref=dst_ref, send_sem=send, recv_sem=recv,
            device_id={"sub": s + dr, "blk": b + dc}, device_id_type=MESH,
        )

    def a_copy(d):
        dr, dc = DIRS[d]
        if d < 2:
            pair_ = a_row_s.at[d], a_row_r.at[d]
        elif d < 4:
            pair_ = a_col_s.at[d - 2], a_col_r.at[d - 2]
        else:
            pair_ = a_cor_s.at[d - 4], a_cor_r.at[d - 4]
        return remote(*pair_, a_sem.at[0, d], a_sem.at[1, d], dr, dc)

    def b_copy(d):
        dr, dc = DIRS[d]
        pair_ = (b_row_s.at[d], b_row_r.at[d]) if d < 2 else (b_cor_s.at[d - 4], b_cor_r.at[d - 4])
        return remote(*pair_, b_sem.at[0, d], b_sem.at[1, d], dr, dc)

    row_bufs = ((x0_s, x0_r), (f1_s, f1_r), (x1_s, x1_r))

    def row_copy(e, d):
        send, recv = row_bufs[e]
        return remote(send.at[d], recv.at[d], row_sem.at[0, e, d], row_sem.at[1, e, d], DIRS[d][0])

    def row_start(e):
        for d in range(2):
            @pl.when(exists(*DIRS[d]))
            def _():
                row_copy(e, d).start()

    def row_wait(e, put):
        for d in range(2):
            @pl.when(exists(-DIRS[d][0], 0))
            def _():
                row_copy(e, d).wait_recv()
                put(d)

    def gather_copy(e, other, sender):
        buf = (cg2_g, f2_g)[e]
        return pltpu.make_async_remote_copy(
            src_ref=buf.at[sender], dst_ref=buf.at[sender],
            send_sem=gather_sem.at[0, e, other], recv_sem=gather_sem.at[1, e, sender],
            device_id={"sub": other}, device_id_type=MESH,
        )

    def gather_start(e):
        for other in range(n_sub):
            @pl.when(s != other)
            def _():
                gather_copy(e, other, s).start()

    def row_done(e):
        for d in range(2):
            @pl.when(exists(*DIRS[d]))
            def _():
                row_copy(e, d).wait_send()

    def gather_done(e):
        for other in range(n_sub):
            @pl.when(s != other)
            def _():
                gather_copy(e, other, s).wait_send()

    def gather_wait(e):
        for other in range(n_sub):
            @pl.when(s != other)
            def _():
                gather_copy(e, other, other).wait_recv()

    def a_start(which):
        for d in which:
            @pl.when(exists(*DIRS[d]))
            def _():
                a_copy(d).start()

    a_start((0, 1))
    for j, lanes in enumerate(sides):
        for k, v in enumerate((c, g, f)):
            a_col_s[j, 16 * k : 16 * k + 16] = v[:, lanes]
    a_start((2, 3))
    for i in range(2):
        for j, lanes in enumerate(sides):
            stage(a_cor_s.at[2 * i + j], *edges[i], lanes)
    a_start((4, 5, 6, 7))
    c0[4:20, halo : halo + own] = c
    g0[4:20, halo : halo + own] = g
    f0[4:20, halo : halo + own] = f

    h1, own1 = halo // 2, own // 2
    both = jnp.concatenate([0.25 * c, g], axis=0)
    both = jnp.concatenate(coarsen(both, tmp), axis=1)
    c1[4:12, h1 : h1 + own1] = both[0:8]
    g1[4:12, h1 : h1 + own1] = both[8:16]
    for i, (rc, rg) in enumerate(((slice(0, 3), slice(8, 10)), (slice(5, 8), slice(14, 16)))):
        b_row_s[i, 0:3] = both[rc]
        b_row_s[i, 3:5] = both[rg]
        b_row_s[i, 5:8] = jnp.zeros((3, own1), jnp.float32)
        for j, lanes in enumerate((slice(0, h1), slice(own1 - h1, own1))):
            b_cor_s[2 * i + j, 0:3] = both[rc, lanes]
            b_cor_s[2 * i + j, 3:5] = both[rg, lanes]
            b_cor_s[2 * i + j, 5:8] = jnp.zeros((3, h1), jnp.float32)
    for d in (0, 1, 4, 5, 6, 7):
        @pl.when(exists(*DIRS[d]))
        def _():
            b_copy(d).start()

    for d, (dr, dc) in enumerate(DIRS):
        @pl.when(exists(-dr, -dc))
        def _():
            a_copy(d).wait_recv()
            lanes = {0: slice(halo, halo + own), 1: slice(0, halo), -1: slice(halo + own, w0)}[dc]
            if dr == 0:
                for k, ref in enumerate((c0, g0, f0)):
                    ref[4:20, lanes] = a_col_r[d - 2, 16 * k : 16 * k + 16]
            else:
                got = (a_row_r, d) if d < 2 else (a_cor_r, d - 4)
                got = got[0].at[got[1]]
                c0[slice(1, 4) if dr > 0 else slice(20, 23), lanes] = got[0:3]
                near = slice(2, 4) if dr > 0 else slice(20, 22)
                g0[near, lanes] = got[3:5]
                f0[near, lanes] = got[5:7]

    terms = chebyshev_terms(*SMOOTH)
    op0 = level_operator(c0[...], g0[...], False, spare0)
    f = f0[...]
    x = smooth(op0, f, None, terms, spare0)
    r = residual(op0, f, x, spare0)
    rhs = jnp.concatenate(coarsen(r[4:20], tmp), axis=1)
    f1[4:12, :] = rhs
    f1_s[0] = rhs[0:2]
    f1_s[1] = rhs[6:8]
    row_start(1)
    x0[...] = x
    x0_s[0] = x[4:6]
    x0_s[1] = x[18:20]
    row_start(0)

    sides = (slice(0, halo), slice(halo + own, w0))
    both = jnp.concatenate(
        [jnp.concatenate([0.25 * c0[4:20, v], g0[4:20, v]], axis=0) for v in sides], axis=1
    )
    both = jnp.concatenate(coarsen(both, tmp), axis=1)
    for k, lanes in enumerate((slice(0, h1), slice(h1 + own1, 2 * h1 + own1))):
        c1[4:12, lanes] = both[0:8, h1 * k : h1 * k + h1]
        g1[4:12, lanes] = both[8:16, h1 * k : h1 * k + h1]
    both = jnp.concatenate([0.25 * c1[4:12, :], g1[4:12, :]], axis=0)
    cg2_g[s] = jnp.concatenate(coarsen(both, tmp), axis=1)
    gather_start(0)
    for d in (0, 1, 4, 5, 6, 7):
        dr, dc = DIRS[d]
        @pl.when(exists(-dr, -dc))
        def _():
            b_copy(d).wait_recv()
            lanes = {0: slice(h1, h1 + own1), 1: slice(0, h1), -1: slice(h1 + own1, w1)}[dc]
            got = b_row_r.at[d] if d < 2 else b_cor_r.at[d - 4]
            c1[slice(1, 4) if dr > 0 else slice(12, 15), lanes] = got[0:3]
            g1[slice(2, 4) if dr > 0 else slice(12, 14), lanes] = got[3:5]
    op1 = level_operator(c1[...], g1[...], False, spare1)

    def put_f1(d):
        f1[slice(12, 14) if d == 0 else slice(2, 4), :] = f1_r[d]

    row_wait(1, put_f1)
    fl1 = f1[...]
    x = smooth(op1, fl1, None, terms, spare1)
    r = residual(op1, fl1, x, spare1)
    f2_g[s] = jnp.concatenate(coarsen(r[4:12], tmp), axis=1)
    gather_start(1)
    x1[...] = x
    x1_s[0] = x[4:7]
    x1_s[1] = x[9:12]
    row_start(2)

    for d in range(8):
        @pl.when(exists(*DIRS[d]))
        def _():
            a_copy(d).wait_send()
            if d not in (2, 3):
                b_copy(d).wait_send()
    row_done(0)
    row_done(1)
    gather_done(0)

    gather_wait(0)
    for k in range(n_sub):
        c2[4 * k : 4 * k + 4, :] = cg2_g[k, 0:4]
        g2[4 * k : 4 * k + 4, :] = cg2_g[k, 4:8]

    cg = (c2[...], g2[...])
    ops = [level_operator(*cg, True)]
    rows = 4 * n_sub
    for level, width in ((3, w3), (4, w4)):
        rows //= 2
        full = max(rows, 8)
        parts = []
        for k, v in enumerate(cg):
            tiles = coarsen(0.25 * v if k == 0 else v, tmp)
            v = jnp.concatenate(tiles, axis=1)[:rows]
            if full > rows:
                v = jnp.concatenate([v, jnp.zeros((full - rows, width), jnp.float32)], axis=0)
            parts.append(v)
        cg = tuple(parts)
        ops.append(level_operator(*cg, True))

    gather_wait(1)
    for k in range(n_sub):
        f2[4 * k : 4 * k + 4, :] = f2_g[k]
    rhs = f2[...]
    kept = []
    rows = 4 * n_sub
    for level in (2, 3):
        op = ops[level - 2]
        x = smooth(op, rhs, None, terms)
        r = residual(op, rhs, x)
        kept.append((rhs, x))
        rows //= 2
        ref = (f3, f4)[level - 2]
        for j, tile in enumerate(coarsen(r, tmp)):
            ref[:rows, 128 * j : 128 * j + 128] = tile
        rhs = ref[...]
    y = smooth(ops[2], rhs, None, chebyshev_terms(coarse_count, COARSE_LOW, COARSE_HIGH))
    for level, width in ((3, w3), (2, w2)):
        op = ops[level - 2]
        rhs, x = kept[level - 2]
        rows = n_sub if level == 3 else 2 * n_sub
        y = x + op[6] * prolong(y, 0, rows, tmp_up, width)
        y = smooth(op, rhs, y, terms)

    for k in range(n_sub):
        y2[k + 1] = y[4 * k : 4 * k + 4]
    y = jnp.concatenate([y2[s][2:4], y2[s + 1], y2[s + 2][0:2]], axis=0)

    def put_x1(d):
        x1[slice(12, 15) if d == 0 else slice(1, 4), :] = x1_r[d]

    row_wait(2, put_x1)
    y = x1[...] + op1[6] * prolong(y, 0, 8, tmp_up, w1)
    y = smooth(op1, fl1, y, terms, spare1)

    def put_x0(d):
        x0[slice(20, 22) if d == 0 else slice(2, 4), :] = x0_r[d]

    row_wait(0, put_x0)
    near = slice(halo - 128, halo + own + 128)
    op0 = [v[:, near] for v in op0]
    y = prolong(y, 2, 12, tmp_up, own + 256, halo // 128 - 1)
    y = smooth(op0, f0[:, near], x0[:, near] + op0[6] * y, terms, spare0)
    out[...] = y[4:20, 128 : 128 + own]

    row_done(2)
    gather_done(1)


def body(conductance, source_mask, ground_mask, nodata_mask):
    n_sub, n_blk = lax.axis_size("sub"), lax.axis_size("blk")
    rows, own = conductance.shape
    assert rows == 16 and own % 256 == 0
    coarse_count = 8 + n_sub // 2
    need = coarse_count + 2
    for _ in range(LEVELS - 1):
        need = 2 * need + 2
    halo = round_up(need, 256)
    assert halo <= own
    w0 = own + 2 * halo
    widths = (w0,) + tuple(round_up(w0 >> l, 128) for l in range(1, 5))
    w1, w2, w3, w4 = widths[1:]
    f32 = lambda *shape: pltpu.VMEM(shape, jnp.float32)
    i32 = lambda *shape: pltpu.VMEM(shape, jnp.int32)
    sem = lambda *shape: pltpu.SemaphoreType.DMA(shape)
    r2, r3, r4 = 4 * n_sub, max(2 * n_sub, 8), max(n_sub, 8)
    tmp_rows = max(32 * w0 // 128, 4 * n_sub * round_up(w2, 256) // 128)
    up_rows = max(24 * w0 // 128, 4 * n_sub * w2 // 128)
    vmem = pl.BlockSpec(memory_space=pltpu.VMEM)
    args = (conductance, source_mask, ground_mask, nodata_mask)
    args = [pltpu.with_memory_space_constraint(v, pltpu.HBM) for v in args]
    return pl.pallas_call(
        functools.partial(kernel, (n_sub, n_blk, halo, widths, coarse_count)),
        out_shape=jax.ShapeDtypeStruct((rows, own), jnp.float32),
        in_specs=[pl.BlockSpec(memory_space=pltpu.HBM)] * 4,
        out_specs=vmem,
        scratch_shapes=[
            f32(rows, own), i32(rows, own), i32(rows, own), i32(rows, own), sem(4),
            f32(w0 // 128, 40, 128), f32(w1 // 128, 32, 128),
            f32(24, w0), f32(24, w0), f32(24, w0), f32(24, w0),
            f32(16, w1), f32(16, w1), f32(16, w1), f32(16, w1),
            f32(r2, w2), f32(r2, w2), f32(r2, w2), f32(n_sub + 2, 4, w2),
            f32(r3, w3), f32(r4, w4), f32(tmp_rows, 128), f32(up_rows, 128),
            f32(2, 8, own), f32(2, 8, own), f32(2, 48, halo), f32(2, 48, halo),
            f32(4, 8, halo), f32(4, 8, halo), sem(2, 8),
            f32(2, 8, own // 2), f32(2, 8, own // 2), f32(4, 8, halo // 2), f32(4, 8, halo // 2), sem(2, 8),
            f32(2, 2, w0), f32(2, 2, w0),
            f32(2, 2, w1), f32(2, 2, w1), f32(2, 3, w1), f32(2, 3, w1), sem(2, 3, 2),
            f32(n_sub, 8, w2), f32(n_sub, 4, w2), sem(2, 2, n_sub),
        ],
        compiler_params=pltpu.CompilerParams(
            collective_id=0, has_side_effects=True, vmem_limit_bytes=40 * 1024 * 1024
        ),
    )(*args)


def solution(mesh):
    spec = P(("groups", "sub"), "blk")
    return jax.shard_map(
        body, mesh=mesh, in_specs=(spec,) * 4, out_specs=spec, check_vma=False
    )
```

```python
import functools
import jax
import jax.numpy as jnp
from jax import lax
from jax.experimental import pallas as pl
from jax.experimental.pallas import tpu as pltpu
from jax.sharding import PartitionSpec as P

LEVELS = 5
SMOOTH = (2, 0.5, 2.0)
COARSE_LOW, COARSE_HIGH = 0.02, 2.0
DIRS = ((-1, 0), (1, 0), (0, -1), (0, 1), (-1, -1), (-1, 1), (1, -1), (1, 1))
MESH = pl.DeviceIdType.MESH


def round_up(n, k):
    return -(-n // k) * k


def chebyshev_terms(sweep_count, low_end, high_end):
    mid = 0.5 * (high_end + low_end)
    half = 0.5 * (high_end - low_end)
    sigma = mid / half
    rho = 1.0 / sigma
    terms = [(0.0, 1.0 / mid)]
    for _ in range(1, sweep_count):
        rho_next = 1.0 / (2.0 * sigma - rho)
        terms.append((rho_next * rho, 2.0 * rho_next / half))
        rho = rho_next
    return terms


def rolled(x, shift, axis):
    return pltpu.roll(x, shift % x.shape[axis], axis)


def level_operator(c, g, whole_rows):
    rows, cols = c.shape
    h = 0.5 * c
    valid = c > 0.0
    c_r = rolled(c, -1, 1)
    c_d = rolled(c, -1, 0)
    e_r = jnp.where(valid & (c_r > 0.0), h + 0.5 * c_r, 0.0)
    ok_d = valid & (c_d > 0.0)
    if whole_rows:
        ok_d = ok_d & (lax.broadcasted_iota(jnp.int32, c.shape, 0) < rows - 1)
    e_d = jnp.where(ok_d, h + 0.5 * c_d, 0.0)
    e_l = rolled(e_r, 1, 1)
    e_u = rolled(e_d, 1, 0)
    m = jnp.where(valid, 1.0, 0.0)
    diag = e_d + e_u + e_r + e_l + g + (1.0 - m)
    inv = 1.0 / jnp.maximum(diag, 0.25 * c)
    return e_r, e_l, e_d, e_u, diag, inv, m


def residual(op, f, x):
    e_r, e_l, e_d, e_u, diag, inv, m = op
    across = e_r * rolled(x, -1, 1) + e_l * rolled(x, 1, 1)
    along = e_d * rolled(x, -1, 0) + e_u * rolled(x, 1, 0)
    return (f - diag * x) + (across + along)


def smooth(op, f, x, terms):
    d = None
    for keep, fresh in terms:
        r = f if x is None else residual(op, f, x)
        step = fresh * (r * op[5])
        d = step if d is None else keep * d + step
        x = d if x is None else x + d
    return x


def lane_take(x, which):
    lane = lax.broadcasted_iota(jnp.int32, x.shape, 1)
    if which == 0:
        index = jnp.bitwise_and(2 * lane, 127)
    else:
        index = jnp.right_shift(lane, 1) + 64 * (which - 1)
    return jnp.take_along_axis(x, index, axis=1, mode="promise_in_bounds")


def coarsen(x, tmp):
    rows, cols = x.shape
    k = round_up(cols, 256) // 256
    half = rows // 2
    sums = []
    for odd in range(2):
        base = odd * rows * k
        for j in range(k):
            lanes = 256 * j + 128 * odd
            if lanes < cols:
                tile = x[:, lanes : lanes + 128]
            else:
                tile = jnp.zeros((rows, 128), jnp.float32)
            tmp[base + rows * j : base + rows * (j + 1), :] = tile
        t = tmp[pl.ds(base, half * k, stride=2), :] + tmp[pl.ds(base + 1, half * k, stride=2), :]
        sums.append(lane_take(t + rolled(t, -1, 1), 0))
    lane = lax.broadcasted_iota(jnp.int32, sums[0].shape, 1)
    s = jnp.where(lane < 64, *sums)
    return [s[half * j : half * (j + 1)] for j in range(k)]


def prolong(x, first, rows, tmp, cols, skip=0):
    n = cols // 128 + skip
    for j in range(x.shape[1] // 128):
        tile = x[:, 128 * j : 128 * j + 128]
        for side in range(2):
            if skip <= 2 * j + side < n:
                base = 2 * rows * (2 * j + side)
                v = lane_take(tile, 1 + side)[first : first + rows]
                tmp[pl.ds(base, rows, stride=2), :] = v
                tmp[pl.ds(base + 1, rows, stride=2), :] = v
    return jnp.concatenate([tmp[2 * rows * j : 2 * rows * (j + 1), :] for j in range(skip, n)], axis=1)


def kernel(
    plan,
    cond_h, src_h, gnd_h, nod_h, out, cond, nod, gnd, src, in_sem,
    c0, g0, f0, x0, c1, g1, f1, x1, c2, g2, f2, y2, f3, f4, tmp, tmp_up,
    a_row_s, a_row_r, a_col_s, a_col_r, a_cor_s, a_cor_r, a_sem,
    b_row_s, b_row_r, b_cor_s, b_cor_r, b_sem,
    x0_s, x0_r, f1_s, f1_r, x1_s, x1_r, row_sem,
    cg2_g, f2_g, gather_sem,
):
    n_sub, n_blk, halo, widths, coarse_count = plan
    s, b = lax.axis_index("sub"), lax.axis_index("blk")
    w0, w1, w2, w3, w4 = widths
    own = out.shape[1]

    def exists(dr, dc):
        ok = None
        for need, cond_ in (
            (dr < 0, s > 0), (dr > 0, s < n_sub - 1), (dc < 0, b > 0), (dc > 0, b < n_blk - 1),
        ):
            if need:
                ok = cond_ if ok is None else ok & cond_
        return ok

    loads = [
        pltpu.make_async_copy(a, v, in_sem.at[i])
        for i, (a, v) in enumerate(((cond_h, cond), (nod_h, nod), (gnd_h, gnd), (src_h, src)))
    ]
    for load in loads:
        load.start()

    barrier = pltpu.get_barrier_semaphore()
    for dr in range(n_sub):
        @pl.when(s != dr)
        def _():
            pl.semaphore_signal(barrier, 1, device_id={"sub": dr}, device_id_type=MESH)
    for dr, dc in DIRS[2:]:
        @pl.when(exists(dr, dc))
        def _():
            pl.semaphore_signal(
                barrier, 1, device_id={"sub": s + dr, "blk": b + dc}, device_id_type=MESH
            )

    for ref in (c0, g0, f0, c1, g1, f1, y2, f3, f4):
        ref[...] = jnp.zeros_like(ref)

    for load in loads:
        load.wait()
    valid = 1.0 - nod[...].astype(jnp.float32)
    c = cond[...] * valid
    g = gnd[...].astype(jnp.float32) * c
    f = valid * (src[...].astype(jnp.float32) - 0.125)
    edges = ((slice(0, 3), slice(0, 2)), (slice(13, 16), slice(14, 16)))
    sides = (slice(0, halo), slice(own - halo, own))

    def stage(ref, rc, rg, lanes):
        ref[0:3] = c[rc, lanes]
        ref[3:5] = g[rg, lanes]
        ref[5:7] = f[rg, lanes]
        ref[7:8] = jnp.zeros((1, ref.shape[1]), jnp.float32)

    for i in range(2):
        stage(a_row_s.at[i], *edges[i], slice(0, own))

    has = lambda flag: jnp.where(flag, 1, 0)
    partners = n_sub - 1
    for dr, dc in DIRS[2:]:
        partners = partners + has(exists(dr, dc))
    pl.semaphore_wait(barrier, partners)

    def remote(src_ref, dst_ref, send, recv, dr, dc=0):
        return pltpu.make_async_remote_copy(
            src_ref=src_ref, dst_ref=dst_ref, send_sem=send, recv_sem=recv,
            device_id={"sub": s + dr, "blk": b + dc}, device_id_type=MESH,
        )

    def a_copy(d):
        dr, dc = DIRS[d]
        if d < 2:
            pair_ = a_row_s.at[d], a_row_r.at[d]
        elif d < 4:
            pair_ = a_col_s.at[d - 2], a_col_r.at[d - 2]
        else:
            pair_ = a_cor_s.at[d - 4], a_cor_r.at[d - 4]
        return remote(*pair_, a_sem.at[0, d], a_sem.at[1, d], dr, dc)

    def b_copy(d):
        dr, dc = DIRS[d]
        pair_ = (b_row_s.at[d], b_row_r.at[d]) if d < 2 else (b_cor_s.at[d - 4], b_cor_r.at[d - 4])
        return remote(*pair_, b_sem.at[0, d], b_sem.at[1, d], dr, dc)

    row_bufs = ((x0_s, x0_r), (f1_s, f1_r), (x1_s, x1_r))

    def row_copy(e, d):
        send, recv = row_bufs[e]
        return remote(send.at[d], recv.at[d], row_sem.at[0, e, d], row_sem.at[1, e, d], DIRS[d][0])

    def row_start(e):
        for d in range(2):
            @pl.when(exists(*DIRS[d]))
            def _():
                row_copy(e, d).start()

    def row_wait(e, put):
        for d in range(2):
            @pl.when(exists(-DIRS[d][0], 0))
            def _():
                row_copy(e, d).wait_recv()
                put(d)

    def gather_copy(e, other, sender):
        buf = (cg2_g, f2_g)[e]
        return pltpu.make_async_remote_copy(
            src_ref=buf.at[sender], dst_ref=buf.at[sender],
            send_sem=gather_sem.at[0, e, other], recv_sem=gather_sem.at[1, e, sender],
            device_id={"sub": other}, device_id_type=MESH,
        )

    def gather_start(e):
        for other in sorted(range(n_sub), key=lambda k: -abs(2 * k - n_sub + 1)):
            @pl.when(s != other)
            def _():
                gather_copy(e, other, s).start()

    def row_done(e):
        for d in range(2):
            @pl.when(exists(*DIRS[d]))
            def _():
                row_copy(e, d).wait_send()

    def gather_done(e):
        for other in range(n_sub):
            @pl.when(s != other)
            def _():
                gather_copy(e, other, s).wait_send()

    def gather_wait(e):
        for other in range(n_sub):
            @pl.when(s != other)
            def _():
                gather_copy(e, other, other).wait_recv()

    def a_start(which):
        for d in which:
            @pl.when(exists(*DIRS[d]))
            def _():
                a_copy(d).start()

    a_start((0, 1))
    for j, lanes in enumerate(sides):
        for k, v in enumerate((c, g, f)):
            a_col_s[j, 16 * k : 16 * k + 16] = v[:, lanes]
    a_start((2, 3))
    for i in range(2):
        for j, lanes in enumerate(sides):
            stage(a_cor_s.at[2 * i + j], *edges[i], lanes)
    a_start((4, 5, 6, 7))
    c0[4:20, halo : halo + own] = c
    g0[4:20, halo : halo + own] = g
    f0[4:20, halo : halo + own] = f

    h1, own1 = halo // 2, own // 2
    both = jnp.concatenate([0.25 * c, g], axis=0)
    both = jnp.concatenate(coarsen(both, tmp), axis=1)
    c1[4:12, h1 : h1 + own1] = both[0:8]
    g1[4:12, h1 : h1 + own1] = both[8:16]
    for i, (rc, rg) in enumerate(((slice(0, 3), slice(8, 10)), (slice(5, 8), slice(14, 16)))):
        b_row_s[i, 0:3] = both[rc]
        b_row_s[i, 3:5] = both[rg]
        b_row_s[i, 5:8] = jnp.zeros((3, own1), jnp.float32)
        for j, lanes in enumerate((slice(0, h1), slice(own1 - h1, own1))):
            b_cor_s[2 * i + j, 0:3] = both[rc, lanes]
            b_cor_s[2 * i + j, 3:5] = both[rg, lanes]
            b_cor_s[2 * i + j, 5:8] = jnp.zeros((3, h1), jnp.float32)
    for d in (0, 1, 4, 5, 6, 7):
        @pl.when(exists(*DIRS[d]))
        def _():
            b_copy(d).start()

    for d, (dr, dc) in enumerate(DIRS):
        @pl.when(exists(-dr, -dc))
        def _():
            a_copy(d).wait_recv()
            lanes = {0: slice(halo, halo + own), 1: slice(0, halo), -1: slice(halo + own, w0)}[dc]
            if dr == 0:
                for k, ref in enumerate((c0, g0, f0)):
                    ref[4:20, lanes] = a_col_r[d - 2, 16 * k : 16 * k + 16]
            else:
                got = (a_row_r, d) if d < 2 else (a_cor_r, d - 4)
                got = got[0].at[got[1]]
                c0[slice(1, 4) if dr > 0 else slice(20, 23), lanes] = got[0:3]
                near = slice(2, 4) if dr > 0 else slice(20, 22)
                g0[near, lanes] = got[3:5]
                f0[near, lanes] = got[5:7]

    terms = chebyshev_terms(*SMOOTH)
    op0 = level_operator(c0[...], g0[...], False)
    f = f0[...]
    x = smooth(op0, f, None, terms)
    r = residual(op0, f, x)
    rhs = jnp.concatenate(coarsen(r[4:20], tmp), axis=1)
    f1[4:12, :] = rhs
    f1_s[0] = rhs[0:2]
    f1_s[1] = rhs[6:8]
    row_start(1)
    x0[...] = x
    x0_s[0] = x[4:6]
    x0_s[1] = x[18:20]
    row_start(0)

    sides = (slice(0, halo), slice(halo + own, w0))
    both = jnp.concatenate(
        [jnp.concatenate([0.25 * c0[4:20, v], g0[4:20, v]], axis=0) for v in sides], axis=1
    )
    both = jnp.concatenate(coarsen(both, tmp), axis=1)
    for k, lanes in enumerate((slice(0, h1), slice(h1 + own1, 2 * h1 + own1))):
        c1[4:12, lanes] = both[0:8, h1 * k : h1 * k + h1]
        g1[4:12, lanes] = both[8:16, h1 * k : h1 * k + h1]
    both = jnp.concatenate([0.25 * c1[4:12, :], g1[4:12, :]], axis=0)
    cg2_g[s] = jnp.concatenate(coarsen(both, tmp), axis=1)
    gather_start(0)
    for d in (0, 1, 4, 5, 6, 7):
        dr, dc = DIRS[d]
        @pl.when(exists(-dr, -dc))
        def _():
            b_copy(d).wait_recv()
            lanes = {0: slice(h1, h1 + own1), 1: slice(0, h1), -1: slice(h1 + own1, w1)}[dc]
            got = b_row_r.at[d] if d < 2 else b_cor_r.at[d - 4]
            c1[slice(1, 4) if dr > 0 else slice(12, 15), lanes] = got[0:3]
            g1[slice(2, 4) if dr > 0 else slice(12, 14), lanes] = got[3:5]
    op1 = level_operator(c1[...], g1[...], False)

    def put_f1(d):
        f1[slice(12, 14) if d == 0 else slice(2, 4), :] = f1_r[d]

    row_wait(1, put_f1)
    fl1 = f1[...]
    x = smooth(op1, fl1, None, terms)
    r = residual(op1, fl1, x)
    f2_g[s] = jnp.concatenate(coarsen(r[4:12], tmp), axis=1)
    gather_start(1)
    x1[...] = x
    x1_s[0] = x[4:7]
    x1_s[1] = x[9:12]
    row_start(2)

    for d in range(8):
        @pl.when(exists(*DIRS[d]))
        def _():
            a_copy(d).wait_send()
            if d not in (2, 3):
                b_copy(d).wait_send()
    row_done(0)
    row_done(1)
    gather_done(0)

    gather_wait(0)
    for k in range(n_sub):
        c2[4 * k : 4 * k + 4, :] = cg2_g[k, 0:4]
        g2[4 * k : 4 * k + 4, :] = cg2_g[k, 4:8]

    cg = (c2[...], g2[...])
    ops = [level_operator(*cg, True)]
    rows = 4 * n_sub
    for level, width in ((3, w3), (4, w4)):
        rows //= 2
        full = max(rows, 8)
        parts = []
        for k, v in enumerate(cg):
            tiles = coarsen(0.25 * v if k == 0 else v, tmp)
            v = jnp.concatenate(tiles, axis=1)[:rows]
            if full > rows:
                v = jnp.concatenate([v, jnp.zeros((full - rows, width), jnp.float32)], axis=0)
            parts.append(v)
        cg = tuple(parts)
        ops.append(level_operator(*cg, True))

    def put_x0(d):
        x0[slice(20, 22) if d == 0 else slice(2, 4), :] = x0_r[d]

    row_wait(0, put_x0)
    def put_x1(d):
        x1[slice(12, 15) if d == 0 else slice(1, 4), :] = x1_r[d]

    row_wait(2, put_x1)

    gather_wait(1)
    for k in range(n_sub):
        f2[4 * k : 4 * k + 4, :] = f2_g[k]
    rhs = f2[...]
    kept = []
    rows = 4 * n_sub
    for level in (2, 3):
        op = ops[level - 2]
        x = smooth(op, rhs, None, terms)
        r = residual(op, rhs, x)
        kept.append((rhs, x))
        rows //= 2
        ref = (f3, f4)[level - 2]
        for j, tile in enumerate(coarsen(r, tmp)):
            ref[:rows, 128 * j : 128 * j + 128] = tile
        rhs = ref[...]
    y = smooth(ops[2], rhs, None, chebyshev_terms(coarse_count, COARSE_LOW, COARSE_HIGH))
    for level, width in ((3, w3), (2, w2)):
        op = ops[level - 2]
        rhs, x = kept[level - 2]
        rows = n_sub if level == 3 else 2 * n_sub
        y = x + op[6] * prolong(y, 0, rows, tmp_up, width)
        y = smooth(op, rhs, y, terms)

    for k in range(n_sub):
        y2[k + 1] = y[4 * k : 4 * k + 4]
    y = jnp.concatenate([y2[s][2:4], y2[s + 1], y2[s + 2][0:2]], axis=0)

    y = x1[...] + op1[6] * prolong(y, 0, 8, tmp_up, w1)
    y = smooth(op1, fl1, y, terms)

    near = slice(halo - 128, halo + own + 128)
    op0 = [v[:, near] for v in op0]
    y = prolong(y, 2, 12, tmp_up, own + 256, halo // 128 - 1)
    y = smooth(op0, f0[:, near], x0[:, near] + op0[6] * y, terms)
    out[...] = y[4:20, 128 : 128 + own]

    row_done(2)
    gather_done(1)


def body(conductance, source_mask, ground_mask, nodata_mask):
    n_sub, n_blk = lax.axis_size("sub"), lax.axis_size("blk")
    rows, own = conductance.shape
    assert rows == 16 and own % 256 == 0
    coarse_count = 8 + n_sub // 2
    need = coarse_count + 2
    for _ in range(LEVELS - 1):
        need = 2 * need + 2
    halo = round_up(need, 256)
    assert halo <= own
    w0 = own + 2 * halo
    widths = (w0,) + tuple(round_up(w0 >> l, 128) for l in range(1, 5))
    w1, w2, w3, w4 = widths[1:]
    f32 = lambda *shape: pltpu.VMEM(shape, jnp.float32)
    i32 = lambda *shape: pltpu.VMEM(shape, jnp.int32)
    sem = lambda *shape: pltpu.SemaphoreType.DMA(shape)
    r2, r3, r4 = 4 * n_sub, max(2 * n_sub, 8), max(n_sub, 8)
    tmp_rows = max(32 * w0 // 128, 4 * n_sub * round_up(w2, 256) // 128)
    up_rows = max(24 * w0 // 128, 4 * n_sub * w2 // 128)
    vmem = pl.BlockSpec(memory_space=pltpu.VMEM)
    args = (conductance, source_mask, ground_mask, nodata_mask)
    args = [pltpu.with_memory_space_constraint(v, pltpu.HBM) for v in args]
    return pl.pallas_call(
        functools.partial(kernel, (n_sub, n_blk, halo, widths, coarse_count)),
        out_shape=jax.ShapeDtypeStruct((rows, own), jnp.float32),
        in_specs=[pl.BlockSpec(memory_space=pltpu.HBM)] * 4,
        out_specs=vmem,
        scratch_shapes=[
            f32(rows, own), i32(rows, own), i32(rows, own), i32(rows, own), sem(4),
            f32(24, w0), f32(24, w0), f32(24, w0), f32(24, w0),
            f32(16, w1), f32(16, w1), f32(16, w1), f32(16, w1),
            f32(r2, w2), f32(r2, w2), f32(r2, w2), f32(n_sub + 2, 4, w2),
            f32(r3, w3), f32(r4, w4), f32(tmp_rows, 128), f32(up_rows, 128),
            f32(2, 8, own), f32(2, 8, own), f32(2, 48, halo), f32(2, 48, halo),
            f32(4, 8, halo), f32(4, 8, halo), sem(2, 8),
            f32(2, 8, own // 2), f32(2, 8, own // 2), f32(4, 8, halo // 2), f32(4, 8, halo // 2), sem(2, 8),
            f32(2, 2, w0), f32(2, 2, w0),
            f32(2, 2, w1), f32(2, 2, w1), f32(2, 3, w1), f32(2, 3, w1), sem(2, 3, 2),
            f32(n_sub, 8, w2), f32(n_sub, 4, w2), sem(2, 2, n_sub),
        ],
        compiler_params=pltpu.CompilerParams(
            collective_id=0, has_side_effects=True, vmem_limit_bytes=40 * 1024 * 1024
        ),
    )(*args)


def solution(mesh):
    spec = P(("groups", "sub"), "blk")
    return jax.shard_map(
        body, mesh=mesh, in_specs=(spec,) * 4, out_specs=spec, check_vma=False
    )
```
